128 devices in a mesh: lat: 8 (over y, core), lon: 16 (over z, x).
Axes of the slice: x: 4, y: 4, z: 4, core: 2. Of those that a mesh axis runs over, the one named last changes fastest.
Arguments:
- tokens: bfloat16 [64, 256, 1024], P('lat', 'lon'), may hold values from -36 to 36
- shifts: int32 [2], replicated, may hold values from 1 to 7, as said below
- w_qkv: bfloat16 [1024, 3072], replicated, may hold values from -0.1875 to 0.1875
- w_out: bfloat16 [1024, 1024], replicated, may hold values from -0.1875 to 0.1875
- router: bfloat16 [1024, 64], replicated, may hold values from -0.1875 to 0.1875
- expert_ids: int32 [8, 16, 128, 2], P('lat', 'lon'), may hold values from 0 to 63, all different within a row; in each aligned block of 128 rows (0 to 127, 128 to 255, ..., all dimensions but the last counted through in order) at most 6 rows name the same one
- w_gate: bfloat16 [1024, 65536], P(None, ('lat', 'lon')), may hold values from -0.1875 to 0.1875
- w_up: bfloat16 [1024, 65536], P(None, ('lat', 'lon')), may hold values from -0.1875 to 0.1875
- w_down: bfloat16 [65536, 1024], P(('lat', 'lon')), may hold values from -0.1875 to 0.1875
Outputs:
- layer_out: bfloat16 [64, 256, 1024], P('lat', 'lon')
The draws below stay inside these ranges and needn't reach their ends.
Inputs may be any that keep to these rules, and one draw needn't show every extreme that they name: `expert_ids`: each token names two different experts; no expert is named by more than 6 of one device's tokens, a bound that some block reaches. The two shifts differ, and one of them is 7.
All inputs are finite; a program needn't handle non-finite values.
Results may differ from the reference program's by a relative error of at most 0.0095.
Values may be sent and summed in bfloat16 or wider, within the bound.
No kernel may reach another device: no remote copies, remote signals or barrier semaphores. Data moves between devices by JAX's collectives and lax.ppermute only.
A program may use at most 64 MiB of HBM per device.

```python
import math
import jax
import jax.numpy as jnp
import numpy as np
from jax import lax

D = 1024
HEAD = 64
HEADS = 16
FF = 1024
EXPERTS = 64
TOP = 2
WIN = 8
CLAT = 8
CLON = 16
LAT = 64
LON = 256
TOK_DEV = 128
TOKENS = 16384
MOST = 6
PIECE = 512
REPL = 2
N_LAT = 8
N_LON = 16


def draw_tokens(key, part):
    key_base, key_rows, key_cols = jax.random.split(key, 3)
    base = jnp.clip(jax.random.normal(key_base, (LAT, LON, D), jnp.float32), -4.0, 4.0)
    rows = jnp.exp(jax.random.uniform(key_rows, (LAT, LON, 1), jnp.float32, math.log(0.3), math.log(3.0)))
    cols = jnp.exp(jax.random.uniform(key_cols, (D,), jnp.float32, math.log(0.3), math.log(3.0)))
    return (base * rows * cols).astype(jnp.bfloat16)


def draw_shifts(key, part):
    key_order, key_other = jax.random.split(jax.random.fold_in(key, 71), 2)
    order = jax.random.randint(key_order, (), 0, 2, dtype=jnp.int32)
    other = jax.random.randint(key_other, (), 1, WIN - 1, dtype=jnp.int32)
    top_shift = jnp.int32(WIN - 1)
    first = jnp.where(order == 0, top_shift, other)
    second = jnp.where(order == 0, other, top_shift)
    return jnp.stack([first, second]).astype(jnp.int32)


def block_levels(rng, shape, cuts, smallest, top_value):
    level = 1.0
    for axis_at, shards_of in cuts:
        draws = jax.random.uniform(jax.random.fold_in(jax.random.fold_in(rng, 6), axis_at), (shards_of,), jnp.float32, smallest / len(cuts), top_value / len(cuts))
        level = level * jnp.repeat(jnp.exp(draws), shape[axis_at] // shards_of).reshape((-1,) + (1,) * (len(shape) - 1 - axis_at))
    return level


def shared_out(own_key, own, number, rows, amount, top, most, skew):
    ranking = jax.random.permutation(own_key, amount)
    packed, usual = portions_of(amount, rows * top, most, skew, True), portions_of(amount, rows * top, most, skew, False)
    places = jnp.arange(amount)

    def named(tallies, rotation):
        used = int((tallies > 0).sum())
        fixed = max(1, used // 4)
        moved = fixed + (places - fixed + rotation * (used - fixed)) % max(1, amount - fixed)
        return jnp.zeros((amount,), jnp.int32).at[ranking[jnp.where(places < fixed, places, moved)]].set(jnp.asarray(tallies, jnp.int32))

    tallies = jnp.where(number % 4 == 0, named(packed, number // 4), named(usual, number - number // 4 - 1))
    mixed = jax.random.permutation(jax.random.fold_in(own, 3), amount)
    giver, sink = mixed[0:amount // 2 * 2:2], mixed[1:amount // 2 * 2:2]
    margin = jnp.minimum(tallies[giver] - 1, most - tallies[sink]) // 2
    margin = jnp.where((giver == ranking[0]) | (sink == ranking[0]) | (tallies[sink] == 0), 0, jnp.maximum(margin, 0))
    moved = jax.random.randint(jax.random.fold_in(own, 4), (amount // 2,), 0, 1 << 20) % (margin + 1)
    tallies = tallies.at[giver].add(-moved).at[sink].add(moved)
    members = jnp.searchsorted(jnp.cumsum(tallies), jnp.arange(rows * top), side="right").astype(jnp.int32)
    table = members.reshape(top, rows).T
    table = table[jax.random.permutation(jax.random.fold_in(own, 1), rows)]
    rotation = jax.random.randint(jax.random.fold_in(own, 2), (rows, 1), 0, top)
    return jnp.take_along_axis(table, (jnp.arange(top)[None, :] + rotation) % top, axis=1)


def portions_of(count, total, most, skew, full):
    weights = [(1 << 20) // math.isqrt(standing ** skew) + 1 for standing in range(1, count + 1)]
    largest = most if full else min(most, max(-(-total // count), total * weights[0] // sum(weights)))
    least = 1 if total - largest >= count - 1 else 0
    given, rest = [largest] + [least] * (count - 1), total - largest - least * (count - 1)
    while rest > 0:
        free = [i for i in range(1, count) if given[i] < largest] or [i for i in range(1, count) if given[i] < most]
        pool, left = sum([weights[i] for i in free]), rest
        for i in free:
            more = min(most - given[i], max(1, left * weights[i] // pool), rest)
            given[i] = given[i] + more
            rest = rest - more
    return np.array(given)


def centred(stream_key, dims, deviation, most, cuts=(), kind=jnp.bfloat16):
    values = jax.random.normal(stream_key, dims, jnp.float32) * deviation
    if len(cuts) > 0:
        values = block_levels(stream_key, dims, cuts, -0.22, 0.18) * values
    return jnp.clip(values, min=-most, max=most).astype(kind)


def setup_inputs(seed: int = 0) -> dict:
    seeds = jax.random.split(jax.random.key(seed), 10)
    tokens = draw_tokens(jax.random.fold_in(seeds[9], 71), 0)
    shifts = draw_shifts(jax.random.fold_in(seeds[9], 71), 0)
    w_qkv = centred(seeds[2], (D, 3 * D), D ** -0.5, 0.1875)
    w_out = centred(seeds[3], (D, D), D ** -0.5, 0.1875)
    router = centred(seeds[4], (D, EXPERTS), D ** -0.5, 0.1875)
    expert_ids_keys = jax.random.split(jax.random.fold_in(seeds[5], 1), N_LAT * N_LON * TOK_DEV // TOK_DEV)
    expert_ids_turns = jax.random.permutation(jax.random.fold_in(seeds[5], 3), N_LAT * N_LON * TOK_DEV // TOK_DEV)
    expert_ids = jax.vmap(lambda own, number: shared_out(jax.random.fold_in(seeds[5], 2), own, number, TOK_DEV, EXPERTS, TOP, MOST, 2))(expert_ids_keys, expert_ids_turns).reshape((N_LAT, N_LON, TOK_DEV, TOP))
    w_gate = centred(seeds[6], (D, EXPERTS * FF), D ** -0.5, 0.1875, ((1, 128),))
    w_up = centred(seeds[7], (D, EXPERTS * FF), D ** -0.5, 0.1875, ((1, 128),))
    w_down = centred(seeds[8], (EXPERTS * FF, D), FF ** -0.5, 0.1875, ((0, 128),))
    return dict(tokens=tokens, shifts=shifts, w_qkv=w_qkv, w_out=w_out, router=router, expert_ids=expert_ids, w_gate=w_gate, w_up=w_up, w_down=w_down)


block_rows = 256

def rms_rows(x):
    xf = x.astype(jnp.float32)
    return xf * lax.rsqrt(lax.optimization_barrier(jnp.mean(xf * xf, axis=-1, keepdims=True)) + 1e-05)

def window_attention(qkv, key_valid):
    query = qkv[:, :, 0]
    keys = qkv[:, :, 1]
    values = qkv[:, :, 2]
    qn = rms_rows(query).astype(jnp.bfloat16)
    kn = rms_rows(keys).astype(jnp.bfloat16)
    scores = jnp.einsum('wqhd,wkhd->whqk', qn.astype(jnp.float32), kn.astype(jnp.float32)) / jnp.sqrt(jnp.float32(HEAD))
    expd = jnp.exp(scores) * key_valid[:, None, None, :]
    total = lax.optimization_barrier(jnp.sum(expd, axis=-1, keepdims=True))
    total = jnp.where(total > 0, total, 1.0)
    weights = (expd / total).astype(jnp.bfloat16)
    return jnp.einsum('whqk,wkhd->wqhd', weights.astype(jnp.float32), values.astype(jnp.float32)).astype(jnp.bfloat16)

def reference(tokens, shifts, w_qkv, w_out, router, expert_ids, w_gate, w_up, w_down):
    s_lat = shifts[0].astype(jnp.int32)
    s_lon = shifts[1].astype(jnp.int32)
    zero = jnp.int32(0)
    normed = rms_rows(tokens).astype(jnp.bfloat16)
    rolled = jnp.roll(normed, s_lon, axis=1)
    padded = lax.dynamic_update_slice(jnp.zeros((LAT + WIN, LON, D), jnp.bfloat16), rolled, (s_lat, zero, zero))
    lat_rows = jnp.arange(LAT + WIN, dtype=jnp.int32)
    valid = ((lat_rows >= s_lat) & (lat_rows < s_lat + LAT)).astype(jnp.float32)
    nbands = (LAT + WIN) // WIN
    wcols = LON // WIN
    bands = padded.reshape(nbands, WIN, LON, D)
    band_valid = valid.reshape(nbands, WIN)

    def band_attention(args):
        band, rows_valid = args
        qkv = jnp.dot(band.reshape(-1, D), w_qkv, preferred_element_type=jnp.float32).astype(jnp.bfloat16)
        qkv = qkv.reshape(WIN, wcols, WIN, 3, HEADS, HEAD).transpose(1, 0, 2, 3, 4, 5).reshape(wcols, WIN * WIN, 3, HEADS, HEAD)
        key_valid = jnp.broadcast_to(rows_valid[None, :, None], (wcols, WIN, WIN)).reshape(wcols, WIN * WIN)
        attended = window_attention(qkv, key_valid)
        return attended.reshape(wcols, WIN, WIN, D).transpose(1, 0, 2, 3).reshape(WIN, LON, D)
    out_bands = lax.map(band_attention, (bands, band_valid)).reshape(LAT + WIN, LON, D)
    attended = lax.dynamic_slice(out_bands, (s_lat, zero, zero), (LAT, LON, D))
    attended = jnp.roll(attended, -s_lon, axis=1).reshape(TOKENS, D)
    projected = jnp.dot(attended, w_out, preferred_element_type=jnp.float32)
    mixed = (tokens.reshape(TOKENS, D).astype(jnp.float32) + projected).astype(jnp.bfloat16)
    normed2 = rms_rows(mixed).astype(jnp.bfloat16)
    logits = jnp.dot(normed2, router, preferred_element_type=jnp.float32)
    ids = expert_ids.reshape(N_LAT, N_LON, CLAT, CLON, TOP).transpose(0, 2, 1, 3, 4).reshape(TOKENS, TOP).astype(jnp.int32)
    chosen = jnp.take_along_axis(logits, ids, axis=1)
    sig = jax.nn.sigmoid(chosen)
    gates = sig / lax.optimization_barrier(jnp.sum(sig, axis=1, keepdims=True))
    total_rows = TOKENS * TOP
    flat = ids.reshape(-1)
    counts = lax.optimization_barrier(jnp.sum((flat[:, None] == jnp.arange(EXPERTS, dtype=jnp.int32)[None, :]).astype(jnp.int32), axis=0)).astype(jnp.int32)
    padded_counts = (counts + block_rows - 1) // block_rows * block_rows
    ends = jnp.cumsum(padded_counts).astype(jnp.int32)
    starts = ends - padded_counts
    order = jnp.argsort(flat, stable=True).astype(jnp.int32)
    sorted_ids = flat[order]
    first_sorted = jnp.cumsum(counts).astype(jnp.int32) - counts
    rank_sorted = jnp.arange(total_rows, dtype=jnp.int32) - first_sorted[sorted_ids]
    dest_sorted = starts[sorted_ids] + rank_sorted
    dest = jnp.zeros((total_rows,), jnp.int32).at[order].set(dest_sorted)
    nblocks = -(-total_rows // block_rows) + EXPERTS
    slot_token = jnp.zeros((nblocks * block_rows,), jnp.int32).at[dest].set(jnp.arange(total_rows, dtype=jnp.int32) // TOP)
    block_start = jnp.arange(nblocks, dtype=jnp.int32) * block_rows
    block_expert = jnp.minimum(lax.optimization_barrier(jnp.sum((ends[None, :] <= block_start[:, None]).astype(jnp.int32), axis=1)), EXPERTS - 1).astype(jnp.int32)

    def run_block(index):
        rows_tok = lax.dynamic_slice_in_dim(slot_token, index * block_rows, block_rows)
        rows = normed2[rows_tok]
        expert = block_expert[index]
        total = jnp.zeros((block_rows, D), jnp.float32)
        for piece in range(REPL):
            start = (expert * FF + piece * PIECE).astype(jnp.int32)
            gate_cols = lax.dynamic_slice_in_dim(w_gate, start, PIECE, 1)
            up_cols = lax.dynamic_slice_in_dim(w_up, start, PIECE, 1)
            down_rows = lax.dynamic_slice_in_dim(w_down, start, PIECE, 0)
            gate = jnp.dot(rows, gate_cols, preferred_element_type=jnp.float32)
            upper = jnp.dot(rows, up_cols, preferred_element_type=jnp.float32)
            hidden = (jax.nn.silu(gate) * upper).astype(jnp.bfloat16)
            part = jnp.dot(hidden, down_rows, preferred_element_type=jnp.float32).astype(jnp.bfloat16)
            total = total + part.astype(jnp.float32)
        return total
    outputs = lax.map(run_block, jnp.arange(nblocks, dtype=jnp.int32)).reshape(nblocks * block_rows, D)
    combined = outputs[dest].reshape(TOKENS, TOP, D)
    moe = lax.optimization_barrier(jnp.sum(gates[:, :, None] * combined, axis=1))
    layer_out = (mixed.astype(jnp.float32) + moe).astype(jnp.bfloat16)
    return layer_out.reshape(LAT, LON, D)
```

```python
import functools

import jax
import jax.numpy as jnp
from jax import lax
from jax.experimental import pallas as pl
from jax.experimental.pallas import tpu as pltpu
from jax.sharding import PartitionSpec as P

HEAD = 64
WIN = 8
MOST = 6
D = 1024
MAIN = 768
TAIL = 256
BLK = 256
BF16 = jnp.bfloat16
F32 = jnp.float32
AXES = ("lat", "lon")


def iota(shape, dim):
    return lax.broadcasted_iota(jnp.int32, shape, dim)


def dot(a, b):
    return jnp.dot(a, b, preferred_element_type=F32)


def rms(x):
    return x * lax.rsqrt(jnp.mean(x * x, axis=-1, keepdims=True) + 1e-05)


def head_norm(y):
    n = y.shape[1]
    square = y * y
    high = square.astype(BF16)
    low = (square - high.astype(F32)).astype(BF16)
    same = jnp.where(iota((n, n), 0) // HEAD == iota((n, n), 1) // HEAD, 1.0, 0.0).astype(BF16)
    total = dot(high, same) + dot(low, same)
    return (y * lax.rsqrt(total * (1.0 / HEAD) + 1e-05)).astype(BF16)


def own_kernel(x_ref, wq_ref, wk_ref, wv_ref, q_ref, k_ref, v_ref, xn):
    @pl.when(pl.program_id(0) == 0)
    def _():
        xn[...] = rms(x_ref[...].astype(F32)).astype(BF16)

    x = xn[...]
    q_ref[...] = head_norm(dot(x, wq_ref[...]).astype(BF16).astype(F32))
    k_ref[...] = head_norm(dot(x, wk_ref[...]).astype(BF16).astype(F32))
    v_ref[...] = dot(x, wv_ref[...]).astype(BF16)


def own_qkv(x, w_qkv):
    n = x.shape[0]
    steps = D // BLK
    col = lambda part: pl.BlockSpec((D, BLK), lambda i: (0, part * steps + i))
    out = pl.BlockSpec((n, BLK), lambda i: (0, i))
    return pl.pallas_call(
        own_kernel,
        grid=(steps,),
        in_specs=[pl.BlockSpec((n, D), lambda i: (0, 0)), col(0), col(1), col(2)],
        out_specs=[out, out, out],
        out_shape=[jax.ShapeDtypeStruct((n, D), BF16)] * 3,
        scratch_shapes=[pltpu.VMEM((n, D), BF16)],
        compiler_params=pltpu.CompilerParams(vmem_limit_bytes=32 << 20),
        cost_estimate=pl.CostEstimate(
            flops=2 * n * D * 3 * D, bytes_accessed=7 << 20, transcendentals=0
        ),
        name="own_qkv",
    )(x, w_qkv, w_qkv, w_qkv)


def route_kernel(experts, ids_ref, idt_ref, pack_ref, pick_ref, spread_ref, gather_ref):
    n = ids_ref.shape[0]
    expert = iota((experts, n), 0)
    first = idt_ref[0:1, :] == expert
    second = idt_ref[1:2, :] == expert
    both = jnp.where(first | second, 1.0, 0.0)
    before = jnp.where(iota((n, n), 0) < iota((n, n), 1), 1.0, 0.0).astype(BF16)
    count = dot(both.astype(BF16), before)
    codes = [
        jnp.sum(jnp.where(hit, count + 8.0 * expert.astype(F32), 0.0), axis=0, keepdims=True)
        for hit in (first, second)
    ]
    rows = 8 * experts
    slot = iota((rows, n), 0)
    base = slot // 8 * 8
    rank = slot % 8
    slot_f = slot.astype(F32)
    main = jnp.where((slot_f == codes[0]) | (slot_f == codes[1]), 1.0, 0.0).astype(BF16)
    for j in range(3):
        want = jnp.where(rank == 6, base + j, jnp.where(rank == 7, base + 3 + j, -1)).astype(F32)
        pack_ref[j, :, 0:n] = main
        pack_ref[j, :, n : 2 * n] = jnp.where(
            (want == codes[0]) | (want == codes[1]), 1.0, 0.0
        ).astype(BF16)
    expert = iota((n, experts), 1)
    first = ids_ref[:, 0:1] == expert
    second = ids_ref[:, 1:2] == expert
    both = jnp.where(first | second, 1.0, 0.0)
    before = jnp.where(iota((n, n), 1) < iota((n, n), 0), 1.0, 0.0).astype(BF16)
    count = dot(before, both.astype(BF16))
    lanes = 16 * experts
    slot = iota((1, lanes), 1)
    base = slot // 16 * 8
    rank = slot % 8
    for k, hit in enumerate((first, second)):
        code = jnp.sum(jnp.where(hit, count + 8.0 * expert.astype(F32), 0.0), axis=1, keepdims=True)
        wants = [jnp.where(rank < MOST, base + rank, -1)]
        for j in range(3):
            wants.append(jnp.where(rank == 6, base + j, jnp.where(rank == 7, base + 3 + j, -1)))
        for j, want in enumerate(wants):
            pick_ref[j, k * n : (k + 1) * n, :] = jnp.where(
                want.astype(F32) == code, 1.0, 0.0
            ).astype(BF16)
    row = iota((BLK, BLK), 0)
    column = iota((BLK, BLK), 1)
    rank = row % 8
    base = row - rank
    for j in range(3):
        source = jnp.where(
            rank == j, base + 6, jnp.where(rank == 3 + j, base + 7, -1)
        )
        spread_ref[:, j * BLK : (j + 1) * BLK] = jnp.where(source == column, 1.0, 0.0).astype(BF16)
        source = jnp.where(rank == 6, base + j, jnp.where(rank == 7, base + 3 + j, -1))
        gather_ref[j * BLK : (j + 1) * BLK, :] = jnp.where(source == column, 1.0, 0.0).astype(BF16)


def route(ids, experts):
    n = ids.shape[0]
    return pl.pallas_call(
        functools.partial(route_kernel, experts),
        out_shape=[
            jax.ShapeDtypeStruct((3, 8 * experts, 2 * n), BF16),
            jax.ShapeDtypeStruct((4, 2 * n, 16 * experts), BF16),
            jax.ShapeDtypeStruct((BLK, 3 * BLK), BF16),
            jax.ShapeDtypeStruct((3 * BLK, BLK), BF16),
        ],
        compiler_params=pltpu.CompilerParams(vmem_limit_bytes=32 << 20),
        cost_estimate=pl.CostEstimate(flops=1 << 28, bytes_accessed=4 << 20, transcendentals=0),
        name="route",
    )(ids, ids.T)


def attend_kernel(
    meta_ref, x_ref, up_ref, down_ref, left_ref, right_ref, ul_ref, ur_ref, dl_ref, dr_ref,
    q_ref, k_ref, v_ref, wk_ref, wv_ref, wo_ref, router_ref, ids_ref, pack_ref,
    mixed_ref, gates_ref, send_ref, xh, acc, mask,
):
    step = pl.program_id(0)
    cut_lat = WIN - meta_ref[0]
    cut_lon = WIN - meta_ref[1]
    n = x_ref.shape[0]
    cols = 16

    @pl.when(step == 0)
    def _():
        def normed(a):
            return rms(a).astype(BF16)

        band = iota((n, 1), 0) // cols >= cut_lat
        xh[0:n, :] = normed(
            jnp.where(band, up_ref[...].astype(F32), down_ref[...].astype(F32))
        )
        cell = iota((64, 1), 0)
        from_left = cell % WIN >= cut_lon
        xh[n : n + 64, :] = normed(
            jnp.where(from_left, left_ref[...].astype(F32), right_ref[...].astype(F32))
        )
        upper = jnp.where(from_left, ul_ref[...].astype(F32), ur_ref[...].astype(F32))
        lower = jnp.where(from_left, dl_ref[...].astype(F32), dr_ref[...].astype(F32))
        xh[n + 64 :, :] = normed(jnp.where(cell // WIN >= cut_lat, upper, lower))
        cell = iota((n, 3 * n), 0)
        row_of = (cell // cols >= cut_lat).astype(jnp.int32)
        col_of = (cell % cols + (WIN - cut_lon)) // WIN
        query = row_of * 3 + col_of
        key = iota((n, 3 * n), 1)
        in_band = (key >= n) & (key < 2 * n)
        in_side = (key >= 2 * n) & (key < 2 * n + 64)
        in_corner = key >= 2 * n + 64
        local = key % n
        small = key % 64
        row = jnp.where(in_side | in_corner, small // WIN, local // cols)
        past = row >= cut_lat
        halo_row = in_band | in_corner
        key_row = jnp.where(past != halo_row, 1, 0)
        edge_low = meta_ref[2] == 0
        edge_high = meta_ref[2] == meta_ref[3] - 1
        outside = halo_row & ((past & edge_low) | (~past & edge_high))
        key_col = jnp.where(
            in_side | in_corner,
            jnp.where(small % WIN >= cut_lon, 0, 2),
            (local % cols + (WIN - cut_lon)) // WIN,
        )
        same = (key_row * 3 + key_col == query) & ~outside
        valid = jnp.where(same, 1.0, 0.0)
        mask[0:n, :] = valid
        mask[n : 2 * n, :] = valid
        acc[...] = jnp.zeros_like(acc)

    x = xh[...]
    keys = jnp.concatenate(
        [k_ref[...], head_norm(dot(x, wk_ref[...]).astype(BF16).astype(F32))], axis=0
    )
    values = jnp.concatenate([v_ref[...], dot(x, wv_ref[...]).astype(BF16)], axis=0)
    low_half = iota((1, 128), 1) < HEAD
    first = jnp.where(low_half, 1.0, 0.0).astype(BF16)
    second = jnp.where(low_half, 0.0, 1.0).astype(BF16)
    outs = []
    for pair in range(BLK // 128):
        lanes = slice(pair * 128, (pair + 1) * 128)
        q = q_ref[:, lanes]
        qq = jnp.concatenate([q * first, q * second], axis=0)
        scores = lax.dot_general(
            qq, keys[:, lanes], (((1,), (1,)), ((), ())), preferred_element_type=F32
        )
        weight = jnp.exp(scores * 0.125) * mask[...]
        weight = weight * (1.0 / jnp.sum(weight, axis=1, keepdims=True))
        out = dot(weight.astype(BF16), values[:, lanes])
        outs.append(jnp.where(low_half, out[0:n], out[n:]).astype(BF16))
    acc[...] += dot(jnp.concatenate(outs, axis=1), wo_ref[...])

    @pl.when(step == pl.num_programs(0) - 1)
    def _():
        mixed = (x_ref[...].astype(F32) + acc[...]).astype(BF16)
        mixed_ref[...] = mixed
        normed = rms(mixed.astype(F32)).astype(BF16)
        logits = dot(normed, router_ref[...])
        expert = iota(logits.shape, 1)
        sig = [
            jax.nn.sigmoid(
                jnp.sum(
                    jnp.where(ids_ref[:, k : k + 1] == expert, logits, 0.0), axis=1, keepdims=True
                )
            )
            for k in range(2)
        ]
        total = sig[0] + sig[1]
        gates_ref[...] = jnp.where(iota((n, 128), 1) == 0, sig[0] / total, sig[1] / total)
        tail = normed[:, MAIN:]
        experts = logits.shape[1]
        for j in range(3):
            lanes = slice(j * BLK, (j + 1) * BLK)
            rows = dot(pack_ref[j], jnp.concatenate([normed[:, lanes], tail], axis=0))
            rows = jnp.broadcast_to(rows.reshape(experts, 1, 8, BLK), (experts, 2, 8, BLK))
            send_ref[:, lanes] = rows.reshape(experts * 16, BLK).astype(BF16)


def attend(meta, x, halo, qkv, w_qkv, w_out, router, ids, pack):
    n = x.shape[0]
    steps = D // BLK
    experts = router.shape[1]
    whole = lambda a: pl.BlockSpec(a.shape, lambda i: (0,) * a.ndim)
    block = pl.BlockSpec((n, BLK), lambda i: (0, i))
    col = lambda part: pl.BlockSpec((D, BLK), lambda i: (0, part * steps + i))
    return pl.pallas_call(
        attend_kernel,
        grid=(steps,),
        in_specs=[
            pl.BlockSpec(memory_space=pltpu.SMEM),
            whole(x),
            *[whole(h) for h in halo],
            block, block, block,
            col(1), col(2),
            pl.BlockSpec((BLK, D), lambda i: (i, 0)),
            whole(router), whole(ids), whole(pack),
        ],
        out_specs=[
            pl.BlockSpec((n, D), lambda i: (0, 0)),
            pl.BlockSpec((n, 128), lambda i: (0, 0)),
            pl.BlockSpec((16 * experts, MAIN), lambda i: (0, 0)),
        ],
        out_shape=[
            jax.ShapeDtypeStruct((n, D), BF16),
            jax.ShapeDtypeStruct((n, 128), F32),
            jax.ShapeDtypeStruct((16 * experts, MAIN), BF16),
        ],
        scratch_shapes=[
            pltpu.VMEM((2 * n, D), BF16),
            pltpu.VMEM((n, D), F32),
            pltpu.VMEM((2 * n, 3 * n), F32),
        ],
        compiler_params=pltpu.CompilerParams(vmem_limit_bytes=40 << 20),
        cost_estimate=pl.CostEstimate(flops=3 << 30, bytes_accessed=10 << 20, transcendentals=1 << 20),
        name="attend",
    )(meta, x, *halo, *qkv, w_qkv, w_qkv, w_out, router, ids, pack)


def expert_kernel(r_ref, wg_ref, wu_ref, wd_ref, spread_ref, gather_ref, out_ref):
    tail = dot(spread_ref[:, 0:BLK], r_ref[:, 0:BLK])
    for j in range(1, 3):
        lanes = slice(j * BLK, (j + 1) * BLK)
        tail = tail + dot(spread_ref[:, lanes], r_ref[:, lanes])
    x = jnp.concatenate([r_ref[...], tail.astype(BF16)], axis=1)
    gate = dot(x, wg_ref[...])
    upper = dot(x, wu_ref[...])
    hidden = (jax.nn.silu(gate) * upper).astype(BF16)
    part = dot(hidden, wd_ref[...]).astype(BF16)
    packed = dot(gather_ref[...], part[:, MAIN:])
    kept = iota((BLK, 1), 0) % 8 < MOST
    for j in range(3):
        lanes = slice(j * BLK, (j + 1) * BLK)
        out_ref[:, lanes] = jnp.where(
            kept, part[:, lanes].astype(F32), packed[lanes, :]
        ).astype(BF16)


def run_experts(received, w_gate, w_up, w_down, spread, gather):
    rows = received.shape[0]
    whole = lambda a: pl.BlockSpec(a.shape, lambda i: (0, 0))
    block = pl.BlockSpec((BLK, MAIN), lambda i: (i, 0))
    return pl.pallas_call(
        expert_kernel,
        grid=(rows // BLK,),
        in_specs=[block, *[whole(a) for a in (w_gate, w_up, w_down, spread, gather)]],
        out_specs=block,
        out_shape=jax.ShapeDtypeStruct(received.shape, BF16),
        compiler_params=pltpu.CompilerParams(vmem_limit_bytes=40 << 20),
        cost_estimate=pl.CostEstimate(flops=4 << 30, bytes_accessed=7 << 20, transcendentals=1 << 19),
        name="experts",
    )(received, w_gate, w_up, w_down, spread, gather)


def combine_kernel(back_ref, pick_ref, gates_ref, mixed_ref, out_ref):
    n = mixed_ref.shape[0]
    gates = [gates_ref[:, 0:1], gates_ref[:, 1:2]]

    def finish(lanes, both):
        moe = gates[0] * both[0:n] + gates[1] * both[n:]
        out_ref[:, lanes] = (mixed_ref[:, lanes].astype(F32) + moe).astype(BF16)

    tail = None
    for j in range(3):
        lanes = slice(j * BLK, (j + 1) * BLK)
        back = back_ref[:, lanes]
        finish(lanes, dot(pick_ref[0], back))
        more = dot(pick_ref[1 + j], back)
        tail = more if tail is None else tail + more
    finish(slice(MAIN, D), tail)


def combine(back, pick, gates, mixed):
    return pl.pallas_call(
        combine_kernel,
        out_shape=jax.ShapeDtypeStruct(mixed.shape, BF16),
        compiler_params=pltpu.CompilerParams(vmem_limit_bytes=40 << 20),
        cost_estimate=pl.CostEstimate(flops=1 << 30, bytes_accessed=5 << 20, transcendentals=0),
        name="combine",
    )(back, pick, gates, mixed)


def halo_of(tokens):
    n_lat, n_lon = lax.axis_size("lat"), lax.axis_size("lon")
    low, high = tokens[:, :WIN], tokens[:, WIN:]

    def moved(x, down, right):
        pairs = [
            (i * n_lon + j, (i + down) % n_lat * n_lon + (j + right) % n_lon)
            for i in range(n_lat)
            for j in range(n_lon)
        ]
        return lax.ppermute(x, AXES, pairs).reshape(-1, x.shape[-1])

    return [
        moved(tokens, 1, 0),
        moved(tokens, -1, 0),
        moved(high, 0, 1),
        moved(low, 0, -1),
        moved(high, 1, 1),
        moved(low, 1, -1),
        moved(high, -1, 1),
        moved(low, -1, -1),
    ]


def body(tokens, shifts, w_qkv, w_out, router, expert_ids, w_gate, w_up, w_down):
    rows, cols, width = tokens.shape
    x = tokens.reshape(-1, width)
    ids = expert_ids.reshape(-1, 2)
    halo = halo_of(tokens)
    meta = jnp.concatenate(
        [shifts, jnp.stack([lax.axis_index("lat"), jnp.int32(lax.axis_size("lat"))])]
    ).astype(jnp.int32)
    pack, pick, spread, gather = route(ids, router.shape[1])
    qkv = own_qkv(x, w_qkv)
    mixed, gates, send = attend(meta, x, halo, qkv, w_qkv, w_out, router, ids, pack)
    received = lax.all_to_all(send, AXES, split_axis=0, concat_axis=0, tiled=True)
    part = run_experts(received, w_gate, w_up, w_down, spread, gather)
    back = lax.all_to_all(part, AXES, split_axis=0, concat_axis=0, tiled=True)
    return combine(back, pick, gates, mixed).reshape(rows, cols, width)


def solution(mesh):
    placed = (
        P("lat", "lon", None),
        P(),
        P(),
        P(),
        P(),
        P("lat", "lon", None, None),
        P(None, ("lat", "lon")),
        P(None, ("lat", "lon")),
        P(("lat", "lon"), None),
    )
    return jax.shard_map(
        body, mesh=mesh, in_specs=placed, out_specs=P("lat", "lon", None), check_vma=False
    )
```

```python
import functools

import jax
import jax.numpy as jnp
from jax import lax
from jax.experimental import pallas as pl
from jax.experimental.pallas import tpu as pltpu
from jax.sharding import PartitionSpec as P

HEAD = 64
WIN = 8
MOST = 6
D = 1024
MAIN = 768
TAIL = 256
BLK = 256
BF16 = jnp.bfloat16
F32 = jnp.float32
AXES = ("lat", "lon")


def iota(shape, dim):
    return lax.broadcasted_iota(jnp.int32, shape, dim)


def dot(a, b):
    return jnp.dot(a, b, preferred_element_type=F32)


def rms(x):
    return x * lax.rsqrt(jnp.mean(x * x, axis=-1, keepdims=True) + 1e-05)


def head_norm(y):
    n = y.shape[1]
    square = y * y
    high = square.astype(BF16)
    low = (square - high.astype(F32)).astype(BF16)
    same = jnp.where(iota((n, n), 0) // HEAD == iota((n, n), 1) // HEAD, 1.0, 0.0).astype(BF16)
    total = dot(high, same) + dot(low, same)
    return (y * lax.rsqrt(total * (1.0 / HEAD) + 1e-05)).astype(BF16)


def vmem_call(kernel, name, out_shape, operands, flops, scratch=(), spaces=None):
    spaces = spaces or {}
    specs = [
        pl.BlockSpec(memory_space=spaces.get(i, pltpu.VMEM)) for i in range(len(operands))
    ]
    count = sum(a.size * a.dtype.itemsize for a in operands)
    outs = jax.tree.map(lambda _: pl.BlockSpec(memory_space=pltpu.VMEM), out_shape)
    return pl.pallas_call(
        kernel,
        in_specs=specs,
        out_specs=outs,
        out_shape=out_shape,
        scratch_shapes=list(scratch),
        compiler_params=pltpu.CompilerParams(vmem_limit_bytes=16 << 20),
        cost_estimate=pl.CostEstimate(flops=flops, bytes_accessed=count, transcendentals=0),
        name=name,
    )(*operands)


def contract_last(a, b):
    return lax.dot_general(a, b, (((1,), (1,)), ((), ())), preferred_element_type=F32)


def tail_source(rank, base, j):
    return jnp.where(rank == 6, base + j, jnp.where(rank == 7, base + 3 + j, -1))


def split_kernel(x_ref, low_ref, high_ref):
    halves = x_ref[...].astype(F32).reshape(-1, 2, WIN, D)
    low_ref[...] = halves[:, 0].reshape(-1, D).astype(BF16)
    high_ref[...] = halves[:, 1].reshape(-1, D).astype(BF16)


def plan_kernel(
    experts, shifts_ref, idt_ref, pack_ref, cols_ref, mask_ref, pick_ref, spread_ref, gather_ref
):
    n = idt_ref.shape[1]
    cut_lat = WIN - shifts_ref[0]
    cut_lon = WIN - shifts_ref[1]
    expert = iota((experts, n), 0)
    hits = [idt_ref[k : k + 1, :] == expert for k in range(2)]
    both = jnp.where(hits[0] | hits[1], 1.0, 0.0)
    before = jnp.where(iota((n, n), 0) < iota((n, n), 1), 1.0, 0.0).astype(BF16)
    count = dot(both.astype(BF16), before)
    ranks = [jnp.sum(jnp.where(hit, count, 0.0), axis=0, keepdims=True) for hit in hits]
    ids = idt_ref[...].astype(F32)
    codes = [ids[k : k + 1] * 8.0 + ranks[k] for k in range(2)]
    eye = jnp.where(iota((n, n), 0) == iota((n, n), 1), 1.0, 0.0).astype(BF16)
    cell = iota((1, n), 1)
    flags = [
        jnp.where(flag, 1.0, 0.0)
        for flag in (cell >> 4 >= cut_lat, cell & 7 >= cut_lon, cell >> 3 >= cut_lat)
    ]
    lines = jnp.concatenate([ids, *ranks, *flags, jnp.zeros((1, n), F32)], axis=0)
    lined = contract_last(eye, lines.astype(BF16))
    cols_ref[...] = lined
    rows = 8 * experts
    slot = iota((rows, n), 0)
    rank = slot & 7
    base = slot - rank

    def chosen(want):
        want = want.astype(F32)
        return jnp.where((want == codes[0]) | (want == codes[1]), 1.0, 0.0).astype(BF16)

    main = chosen(slot)
    for j in range(3):
        pack_ref[j, :, 0:n] = main
        pack_ref[j, :, n : 2 * n] = chosen(tail_source(rank, base, j))
    cell = iota((n, 1), 0)
    query = jnp.where(cell >> 4 >= cut_lat, 3, 0) + ((cell & 15) + shifts_ref[1] >> 3)
    key = iota((1, 3 * n), 1)
    narrow = key >= 2 * n
    halo_row = ((key >= n) & (key < 2 * n)) | (key >= 2 * n + WIN * WIN)
    past = jnp.where(narrow, key >> 3 & 7, key >> 4 & 7) >= cut_lat
    lat = lax.axis_index("lat")
    first, final = lat == 0, lat == lax.axis_size("lat") - 1
    beyond = halo_row & ((past & first) | (~past & final))
    window = jnp.where(past != halo_row, 3, 0) + jnp.where(
        narrow, jnp.where(key & 7 >= cut_lon, 0, 2), (key & 15) + shifts_ref[1] >> 3
    )
    valid = jnp.where(query == jnp.where(beyond, -1, window), 1.0, 0.0).astype(BF16)
    mask_ref[0:n, :] = valid
    mask_ref[n : 2 * n, :] = valid
    lanes = 16 * experts
    slot = iota((1, lanes), 1)
    base = (slot >> 4) * 8
    rank = slot & 7
    wants = [jnp.where(rank < MOST, base + rank, -1)]
    wants += [tail_source(rank, base, j) for j in range(3)]
    for k in range(2):
        code = lined[:, k : k + 1] * 8.0 + lined[:, 2 + k : 3 + k]
        for j, want in enumerate(wants):
            pick_ref[j, k * n : (k + 1) * n, :] = jnp.where(
                want.astype(F32) == code, 1.0, 0.0
            ).astype(BF16)
    row = iota((BLK, BLK), 0)
    column = iota((BLK, BLK), 1)
    rank = row & 7
    base = row - rank
    for j in range(3):
        lanes = slice(j * BLK, (j + 1) * BLK)
        source = jnp.where(rank == j, base + 6, jnp.where(rank == 3 + j, base + 7, -1))
        spread_ref[:, lanes] = jnp.where(source == column, 1.0, 0.0).astype(BF16)
        source = tail_source(rank, base, j)
        gather_ref[lanes, :] = jnp.where(source == column, 1.0, 0.0).astype(BF16)


def attend_keys(queries, keys, values, mask):
    n = queries.shape[0] // 2
    low_half = iota((1, 128), 1) < HEAD
    weight = jnp.exp(contract_last(queries, keys)).astype(BF16) * mask
    both = dot(weight, jnp.concatenate([values, jnp.ones_like(values)], axis=1))
    return (
        jnp.where(low_half, both[0:n, 0:128], both[n:, 0:128]),
        jnp.where(low_half, both[0:n, 128:], both[n:, 128:]),
    )


def own_kernel(x_ref, w_ref, mask_ref, qq_ref, num_ref, den_ref):
    n = x_ref.shape[0]
    x = rms(x_ref[...].astype(F32)).astype(BF16)
    mask = mask_ref[:, 0:n]
    low_half = iota((1, 128), 1) < HEAD
    for i in range(D // BLK):
        lanes = slice(i * BLK, (i + 1) * BLK)
        q, k, v = [
            dot(x, w_ref[:, part * D + i * BLK : part * D + (i + 1) * BLK]).astype(BF16)
            for part in range(3)
        ]
        q = head_norm(q.astype(F32)).astype(F32) * 0.125
        k = head_norm(k.astype(F32))
        for pair in range(BLK // 128):
            some = slice(pair * 128, (pair + 1) * 128)
            qq = jnp.concatenate(
                [jnp.where(low_half, q[:, some], 0.0), jnp.where(low_half, 0.0, q[:, some])], axis=0
            ).astype(BF16)
            num, den = attend_keys(qq, k[:, some], v[:, some], mask)
            lanes = slice(i * BLK + pair * 128, i * BLK + (pair + 1) * 128)
            qq_ref[:, lanes] = qq
            num_ref[:, lanes] = num
            den_ref[:, lanes] = den


def side_kernel(left_ref, right_ref, cols_ref, side_ref):
    n = side_ref.shape[0]
    side_ref[...] = jnp.where(
        cols_ref[0:n, 5:6] > 0.5, left_ref[...].astype(F32), right_ref[...].astype(F32)
    ).astype(BF16)


def near_kernel(
    up_ref, down_ref, side_ref, w_ref, mask_ref, cols_ref, qq_ref, num_in, den_in, num_ref, den_ref
):
    n = up_ref.shape[0]
    past = cols_ref[:, 4:5] > 0.5
    band = jnp.where(past, up_ref[...].astype(F32), down_ref[...].astype(F32))
    x = jnp.concatenate(
        [rms(band).astype(BF16), rms(side_ref[...].astype(F32)).astype(BF16)], axis=0
    )
    mask = mask_ref[:, n : n + x.shape[0]]
    for i in range(D // BLK):
        k, v = [
            dot(x, w_ref[:, part * D + i * BLK : part * D + (i + 1) * BLK]).astype(BF16)
            for part in (1, 2)
        ]
        k = head_norm(k.astype(F32))
        for pair in range(BLK // 128):
            some = slice(pair * 128, (pair + 1) * 128)
            lanes = slice(i * BLK + pair * 128, i * BLK + (pair + 1) * 128)
            num, den = attend_keys(qq_ref[:, lanes], k[:, some], v[:, some], mask)
            num_ref[:, lanes] = num_in[:, lanes] + num
            den_ref[:, lanes] = den_in[:, lanes] + den


def last_kernel(
    x_ref, up_ref, down_ref, w_ref, mask_ref, qq_ref, num_ref, den_ref,
    wo_ref, router_ref, cols_ref, pack_ref, mixed_ref, gates_ref, send_ref,
):
    n = x_ref.shape[0]
    m = up_ref.shape[0]
    past = cols_ref[0:m, 6:7] > 0.5
    corner = jnp.where(past, up_ref[...].astype(F32), down_ref[...].astype(F32))
    x = rms(corner).astype(BF16)
    mask = mask_ref[:, 3 * n - m :]
    total = None
    for i in range(D // BLK):
        k, v = [
            dot(x, w_ref[:, part * D + i * BLK : part * D + (i + 1) * BLK]).astype(BF16)
            for part in (1, 2)
        ]
        k = head_norm(k.astype(F32))
        outs = []
        for pair in range(BLK // 128):
            some = slice(pair * 128, (pair + 1) * 128)
            lanes = slice(i * BLK + pair * 128, i * BLK + (pair + 1) * 128)
            num, den = attend_keys(qq_ref[:, lanes], k[:, some], v[:, some], mask)
            outs.append(((num_ref[:, lanes] + num) / (den_ref[:, lanes] + den)).astype(BF16))
        more = dot(jnp.concatenate(outs, axis=1), wo_ref[i * BLK : (i + 1) * BLK, :])
        total = more if total is None else total + more
    mixed = (x_ref[...].astype(F32) + total).astype(BF16)
    mixed_ref[...] = mixed
    normed = rms(mixed.astype(F32)).astype(BF16)
    logits = contract_last(normed, router_ref[...])
    experts = logits.shape[1]
    expert = iota(logits.shape, 1).astype(F32)
    sig = [
        jax.nn.sigmoid(
            jnp.sum(jnp.where(cols_ref[:, k : k + 1] == expert, logits, 0.0), axis=1, keepdims=True)
        )
        for k in range(2)
    ]
    gates_ref[...] = jnp.where(iota((n, 128), 1) == 0, sig[0], sig[1]) / (sig[0] + sig[1])
    for j in range(3):
        lanes = slice(j * BLK, (j + 1) * BLK)
        rows = dot(pack_ref[j], jnp.concatenate([normed[:, lanes], normed[:, MAIN:]], axis=0))
        rows = jnp.broadcast_to(rows.reshape(experts, 1, 8, BLK), (experts, 2, 8, BLK))
        send_ref[:, lanes] = rows.reshape(experts * 16, BLK).astype(BF16)


def expert_kernel(r_ref, wg_ref, wu_ref, wd_ref, spread_ref, gather_ref, out_ref):
    for block in range(r_ref.shape[0] // BLK):
        rows = slice(block * BLK, (block + 1) * BLK)
        tail = None
        for j in range(3):
            lanes = slice(j * BLK, (j + 1) * BLK)
            more = dot(spread_ref[:, lanes], r_ref[rows, lanes])
            tail = more if tail is None else tail + more
        x = jnp.concatenate([r_ref[rows, :], tail.astype(BF16)], axis=1)
        gate = dot(x, wg_ref[...])
        upper = dot(x, wu_ref[...])
        hidden = (jax.nn.silu(gate) * upper).astype(BF16)
        part = dot(hidden, wd_ref[...]).astype(BF16)
        packed = dot(gather_ref[...], part[:, MAIN:])
        kept = (iota((BLK, 1), 0) & 7) < MOST
        for j in range(3):
            lanes = slice(j * BLK, (j + 1) * BLK)
            out_ref[rows, lanes] = jnp.where(
                kept, part[:, lanes].astype(F32), packed[lanes, :]
            ).astype(BF16)


def combine_kernel(back_ref, pick_ref, gates_ref, mixed_ref, out_ref):
    n = mixed_ref.shape[0]
    gates = [gates_ref[:, 0:1], gates_ref[:, 1:2]]

    def finish(lanes, both):
        moe = gates[0] * both[0:n] + gates[1] * both[n:]
        out_ref[:, lanes] = (mixed_ref[:, lanes].astype(F32) + moe).astype(BF16)

    tail = None
    for j in range(3):
        lanes = slice(j * BLK, (j + 1) * BLK)
        back = back_ref[:, lanes]
        finish(lanes, dot(pick_ref[0], back))
        more = dot(pick_ref[1 + j], back)
        tail = more if tail is None else tail + more
    finish(slice(MAIN, D), tail)


def moved(x, down, right):
    n_lat, n_lon = lax.axis_size("lat"), lax.axis_size("lon")
    pairs = [
        (i * n_lon + j, (i + down) % n_lat * n_lon + (j + right) % n_lon)
        for i in range(n_lat)
        for j in range(n_lon)
    ]
    return lax.ppermute(x, AXES, pairs)


def body(tokens, shifts, w_qkv, w_out, router, expert_ids, w_gate, w_up, w_down):
    rows, cols, width = tokens.shape
    n = rows * cols
    experts = router.shape[1]
    shape = jax.ShapeDtypeStruct
    half = shape((n // 2, width), BF16)
    x = tokens.reshape(n, width)
    low, high = vmem_call(split_kernel, "split", [half, half], (x,), 1 << 20)
    left = moved(high, 0, 1)
    right = moved(low, 0, -1)
    up = moved(x, 1, 0)
    down = moved(x, -1, 0)
    sums = [shape((n, width), F32)] * 2
    pack, cells, mask, pick, spread, gather = vmem_call(
        functools.partial(plan_kernel, experts),
        "plan",
        [
            shape((3, 8 * experts, 2 * n), BF16),
            shape((n, 8), F32),
            shape((2 * n, 3 * n), BF16),
            shape((4, 2 * n, 16 * experts), BF16),
            shape((BLK, MAIN), BF16),
            shape((MAIN, BLK), BF16),
        ],
        (shifts, expert_ids.reshape(n, 2).T),
        3 << 30,
        spaces={0: pltpu.SMEM},
    )
    qq, num, den = vmem_call(
        own_kernel,
        "own",
        [shape((2 * n, width), BF16), *sums],
        (x, w_qkv, mask),
        8 * n * width * width,
    )
    left, right, num = lax.optimization_barrier((left, right, num))
    side = vmem_call(side_kernel, "side", half, (left, right, cells), 1 << 10)
    up_side = moved(side, 1, 0)
    down_side = moved(side, -1, 0)
    num, den = vmem_call(
        near_kernel,
        "near",
        sums,
        (up, down, side, w_qkv, mask, cells, qq, num, den),
        8 * n * width * width,
    )
    mixed, gates, send = vmem_call(
        last_kernel,
        "last",
        [shape((n, width), BF16), shape((n, 128), F32), shape((16 * experts, MAIN), BF16)],
        (x, up_side, down_side, w_qkv, mask, qq, num, den, w_out, router.T, cells, pack),
        6 * n * width * width,
    )
    received = lax.all_to_all(send, AXES, split_axis=0, concat_axis=0, tiled=True)
    part = vmem_call(
        expert_kernel,
        "experts",
        shape(received.shape, BF16),
        (received, w_gate, w_up, w_down, spread, gather),
        1 << 32,
    )
    back = lax.all_to_all(part, AXES, split_axis=0, concat_axis=0, tiled=True)
    out = vmem_call(
        combine_kernel, "combine", shape((n, width), BF16), (back, pick, gates, mixed), 1 << 30
    )
    return out.reshape(rows, cols, width)


def solution(mesh):
    placed = (
        P("lat", "lon", None),
        P(),
        P(),
        P(),
        P(),
        P("lat", "lon", None, None),
        P(None, ("lat", "lon")),
        P(None, ("lat", "lon")),
        P(("lat", "lon"), None),
    )
    return jax.shard_map(
        body, mesh=mesh, in_specs=placed, out_specs=P("lat", "lon", None), check_vma=False
    )
```

```python
import functools

import jax
import jax.numpy as jnp
from jax import lax
from jax.experimental import pallas as pl
from jax.experimental.pallas import tpu as pltpu
from jax.sharding import PartitionSpec as P

HEAD = 64
WIN = 8
MOST = 6
D = 1024
BLK = 256
BF16 = jnp.bfloat16
F32 = jnp.float32
AXES = ("lat", "lon")


def iota(shape, dim):
    return lax.broadcasted_iota(jnp.int32, shape, dim)


def dot(a, b):
    return jnp.dot(a, b, preferred_element_type=F32)


def rms(x):
    return x * lax.rsqrt(jnp.mean(x * x, axis=-1, keepdims=True) + 1e-05)


def head_norm(y):
    n = y.shape[1]
    same = jnp.where(iota((n, n), 0) // HEAD == iota((n, n), 1) // HEAD, 1.0, 0.0).astype(BF16)
    total = dot((y * y).astype(BF16), same)
    return (y * lax.rsqrt(total * (1.0 / HEAD) + 1e-05)).astype(BF16)


def vmem_call(kernel, name, out_shape, operands, flops, scratch=(), spaces=None):
    spaces = spaces or {}
    specs = [
        pl.BlockSpec(memory_space=spaces.get(i, pltpu.VMEM)) for i in range(len(operands))
    ]
    count = sum(a.size * a.dtype.itemsize for a in operands)
    outs = jax.tree.map(lambda _: pl.BlockSpec(memory_space=pltpu.VMEM), out_shape)
    return pl.pallas_call(
        kernel,
        in_specs=specs,
        out_specs=outs,
        out_shape=out_shape,
        scratch_shapes=list(scratch),
        compiler_params=pltpu.CompilerParams(vmem_limit_bytes=16 << 20),
        cost_estimate=pl.CostEstimate(flops=flops, bytes_accessed=count, transcendentals=0),
        name=name,
    )(*operands)


def contract_last(a, b):
    return lax.dot_general(a, b, (((1,), (1,)), ((), ())), preferred_element_type=F32)


def split_kernel(tokens_ref, x_ref, low_ref, high_ref):
    x = tokens_ref[...]
    x_ref[...] = x
    halves = x.astype(F32).reshape(-1, 2, WIN, D)
    low_ref[...] = halves[:, 0].reshape(-1, D).astype(BF16)
    high_ref[...] = halves[:, 1].reshape(-1, D).astype(BF16)


def plan_kernel(experts, shifts_ref, ids_ref, pack_ref, cells_ref, mask_ref, pick_ref):
    n = ids_ref.shape[1]
    shift_lat, shift_lon = shifts_ref[0], shifts_ref[1]
    cut_lat = WIN - shift_lat
    cut_lon = WIN - shift_lon
    expert = iota((experts, n), 0)
    hits = [ids_ref[k : k + 1, :] == expert for k in range(2)]
    both = jnp.where(hits[0] | hits[1], 1.0, 0.0)
    before = jnp.where(iota((n, n), 0) < iota((n, n), 1), 1.0, 0.0).astype(BF16)
    count = dot(both.astype(BF16), before)
    ranks = [jnp.sum(jnp.where(hit, count, 0.0), axis=0, keepdims=True) for hit in hits]
    ids = ids_ref[...].astype(F32)
    cell = iota((1, n), 1)
    flags = [
        jnp.where(flag, 1.0, 0.0)
        for flag in (cell >> 4 >= cut_lat, cell & 7 >= cut_lon, cell >> 3 >= cut_lat)
    ]
    lines = jnp.concatenate([ids, *ranks, *flags, jnp.zeros((1, n), F32)], axis=0)
    eye = jnp.where(iota((n, n), 0) == iota((n, n), 1), 1.0, 0.0).astype(BF16)
    cells = contract_last(eye, lines.astype(BF16))
    cells_ref[...] = cells
    slot = iota((MOST * experts, n), 0).astype(F32)
    codes = [ids[k : k + 1] * MOST + ranks[k] for k in range(2)]
    pack_ref[...] = jnp.where((slot == codes[0]) | (slot == codes[1]), 1.0, 0.0).astype(BF16)
    slot = iota((1, 2 * MOST * experts), 1)
    slot = (slot // (2 * MOST) * MOST + slot % MOST).astype(F32)
    for k in range(2):
        code = cells[:, k : k + 1] * MOST + cells[:, 2 + k : 3 + k]
        pick_ref[k * n : (k + 1) * n, :] = jnp.where(slot == code, 1.0, 0.0).astype(BF16)
    cell = iota((n, 1), 0)
    query = jnp.where(cell >> 4 >= cut_lat, 3, 0) + ((cell & 15) + shift_lon >> 3)
    key = iota((1, 3 * n), 1)
    narrow = key >= 2 * n
    halo_row = ((key >= n) & (key < 2 * n)) | (key >= 2 * n + WIN * WIN)
    past = jnp.where(narrow, key >> 3 & 7, key >> 4 & 7) >= cut_lat
    lat = lax.axis_index("lat")
    first, final = lat == 0, lat == lax.axis_size("lat") - 1
    beyond = halo_row & ((past & first) | (~past & final))
    window = jnp.where(past != halo_row, 3, 0) + jnp.where(
        narrow, jnp.where(key & 7 >= cut_lon, 0, 2), (key & 15) + shift_lon >> 3
    )
    valid = jnp.where(query == jnp.where(beyond, -1, window), 1.0, 0.0).astype(BF16)
    mask_ref[0:n, :] = valid
    mask_ref[n : 2 * n, :] = valid


def attend_keys(queries, keys, values, mask):
    n = queries.shape[0] // 2
    low_half = iota((1, 128), 1) < HEAD
    weight = jnp.exp(contract_last(queries, keys)).astype(BF16) * mask
    both = dot(weight, jnp.concatenate([values, jnp.ones_like(values)], axis=1))
    return (
        jnp.where(low_half, both[0:n, 0:128], both[n:, 0:128]),
        jnp.where(low_half, both[0:n, 128:], both[n:, 128:]),
    )


def own_kernel(x_ref, w_ref, mask_ref, qq_ref, num_ref, den_ref):
    n = x_ref.shape[0]
    x = rms(x_ref[...].astype(F32)).astype(BF16)
    mask = mask_ref[:, 0:n]
    low_half = iota((1, 128), 1) < HEAD
    for i in range(D // BLK):
        lanes = slice(i * BLK, (i + 1) * BLK)
        q, k, v = [
            dot(x, w_ref[:, part * D + i * BLK : part * D + (i + 1) * BLK]).astype(BF16)
            for part in range(3)
        ]
        q = head_norm(q.astype(F32)).astype(F32) * 0.125
        k = head_norm(k.astype(F32))
        for pair in range(BLK // 128):
            some = slice(pair * 128, (pair + 1) * 128)
            qq = jnp.concatenate(
                [jnp.where(low_half, q[:, some], 0.0), jnp.where(low_half, 0.0, q[:, some])], axis=0
            ).astype(BF16)
            num, den = attend_keys(qq, k[:, some], v[:, some], mask)
            lanes = slice(i * BLK + pair * 128, i * BLK + (pair + 1) * 128)
            qq_ref[:, lanes] = qq
            num_ref[:, lanes] = num
            den_ref[:, lanes] = den


def side_kernel(left_ref, right_ref, cells_ref, side_ref):
    n = side_ref.shape[0]
    side_ref[...] = jnp.where(
        cells_ref[0:n, 5:6] > 0.5, left_ref[...].astype(F32), right_ref[...].astype(F32)
    ).astype(BF16)


def near_kernel(
    up_ref, down_ref, side_ref, w_ref, mask_ref, cells_ref, qq_ref, num_in, den_in, num_ref, den_ref
):
    n = up_ref.shape[0]
    past = cells_ref[:, 4:5] > 0.5
    band = jnp.where(past, up_ref[...].astype(F32), down_ref[...].astype(F32))
    x = jnp.concatenate(
        [rms(band).astype(BF16), rms(side_ref[...].astype(F32)).astype(BF16)], axis=0
    )
    mask = mask_ref[:, n : n + x.shape[0]]
    for i in range(D // BLK):
        k, v = [
            dot(x, w_ref[:, part * D + i * BLK : part * D + (i + 1) * BLK]).astype(BF16)
            for part in (1, 2)
        ]
        k = head_norm(k.astype(F32))
        for pair in range(BLK // 128):
            some = slice(pair * 128, (pair + 1) * 128)
            lanes = slice(i * BLK + pair * 128, i * BLK + (pair + 1) * 128)
            num, den = attend_keys(qq_ref[:, lanes], k[:, some], v[:, some], mask)
            num_ref[:, lanes] = num_in[:, lanes] + num
            den_ref[:, lanes] = den_in[:, lanes] + den


def last_kernel(
    x_ref, up_ref, down_ref, w_ref, mask_ref, qq_ref, num_ref, den_ref,
    wo_ref, router_ref, cells_ref, pack_ref, mixed_ref, gates_ref, send_ref,
):
    n = x_ref.shape[0]
    m = up_ref.shape[0]
    past = cells_ref[0:m, 6:7] > 0.5
    corner = jnp.where(past, up_ref[...].astype(F32), down_ref[...].astype(F32))
    x = rms(corner).astype(BF16)
    mask = mask_ref[:, 3 * n - m :]
    total = None
    for i in range(D // BLK):
        k, v = [
            dot(x, w_ref[:, part * D + i * BLK : part * D + (i + 1) * BLK]).astype(BF16)
            for part in (1, 2)
        ]
        k = head_norm(k.astype(F32))
        outs = []
        for pair in range(BLK // 128):
            some = slice(pair * 128, (pair + 1) * 128)
            lanes = slice(i * BLK + pair * 128, i * BLK + (pair + 1) * 128)
            num, den = attend_keys(qq_ref[:, lanes], k[:, some], v[:, some], mask)
            outs.append(((num_ref[:, lanes] + num) / (den_ref[:, lanes] + den)).astype(BF16))
        more = dot(jnp.concatenate(outs, axis=1), wo_ref[i * BLK : (i + 1) * BLK, :])
        total = more if total is None else total + more
    mixed = (x_ref[...].astype(F32) + total).astype(BF16)
    mixed_ref[...] = mixed
    normed = rms(mixed.astype(F32)).astype(BF16)
    logits = contract_last(normed, router_ref[...])
    experts = logits.shape[1]
    expert = iota(logits.shape, 1).astype(F32)
    sig = [
        jax.nn.sigmoid(
            jnp.sum(jnp.where(cells_ref[:, k : k + 1] == expert, logits, 0.0), axis=1, keepdims=True)
        )
        for k in range(2)
    ]
    gates_ref[...] = jnp.where(iota((n, 128), 1) == 0, sig[0], sig[1]) / (sig[0] + sig[1])
    rows = dot(pack_ref[...], normed).astype(BF16).reshape(-1, 8, 128)
    rows = rows.reshape(experts, MOST, 8, 128)
    send_ref[:, 0] = rows
    send_ref[:, 1] = rows


def expert_kernel(rows_ref, wg_ref, wu_ref, wd_ref, out_ref):
    x = rows_ref[...].reshape(-1, D)
    gate = dot(x, wg_ref[...])
    upper = dot(x, wu_ref[...])
    hidden = (jax.nn.silu(gate) * upper).astype(BF16)
    out_ref[...] = dot(hidden, wd_ref[...]).astype(BF16).reshape(out_ref.shape)


def combine_kernel(back_ref, pick_ref, gates_ref, mixed_ref, out_ref):
    n = mixed_ref.shape[0]
    both = dot(pick_ref[...], back_ref[...].reshape(-1, D))
    moe = gates_ref[:, 0:1] * both[0:n] + gates_ref[:, 1:2] * both[n:]
    out_ref[...] = (mixed_ref[...].astype(F32) + moe).astype(BF16)


def moved(x, down, right):
    n_lat, n_lon = lax.axis_size("lat"), lax.axis_size("lon")
    pairs = [
        (i * n_lon + j, (i + down) % n_lat * n_lon + (j + right) % n_lon)
        for i in range(n_lat)
        for j in range(n_lon)
    ]
    return lax.ppermute(x, AXES, pairs)


def body(tokens, shifts, w_qkv, w_out, router, expert_ids, w_gate, w_up, w_down):
    rows, cols, width = tokens.shape
    n = rows * cols
    experts = router.shape[1]
    shape = jax.ShapeDtypeStruct
    half = shape((n // 2, width), BF16)
    cells, ids, shifts = lax.optimization_barrier(
        (tokens.reshape(n, width), expert_ids.reshape(n, 2).T, shifts)
    )
    x, low, high = vmem_call(
        split_kernel, "split", [shape((n, width), BF16), half, half], (cells,), 1 << 20
    )
    left = moved(high, 0, 1)
    right = moved(low, 0, -1)
    up = moved(x, 1, 0)
    down = moved(x, -1, 0)
    sums = [shape((n, width), F32)] * 2
    pack, cells, mask, pick = vmem_call(
        functools.partial(plan_kernel, experts),
        "plan",
        [
            shape((MOST * experts, n), BF16),
            shape((n, 8), F32),
            shape((2 * n, 3 * n), BF16),
            shape((2 * n, 2 * MOST * experts), BF16),
        ],
        (shifts, ids),
        3 << 30,
        spaces={0: pltpu.SMEM},
    )
    qq, num, den = vmem_call(
        own_kernel,
        "own",
        [shape((2 * n, width), BF16), *sums],
        (x, w_qkv, mask),
        8 * n * width * width,
    )
    left, right, num = lax.optimization_barrier((left, right, num))
    side = vmem_call(side_kernel, "side", half, (left, right, cells), 1 << 10)
    up_side = moved(side, 1, 0)
    down_side = moved(side, -1, 0)
    num, den = vmem_call(
        near_kernel,
        "near",
        sums,
        (up, down, side, w_qkv, mask, cells, qq, num, den),
        8 * n * width * width,
    )
    mixed, gates, send = vmem_call(
        last_kernel,
        "last",
        [
            shape((n, width), BF16),
            shape((n, 128), F32),
            shape((experts, 2, MOST, 8, width // 8), BF16),
        ],
        (x, up_side, down_side, w_qkv, mask, qq, num, den, w_out, router.T, cells, pack),
        6 * n * width * width,
    )
    send = send.reshape(2 * experts * MOST, 8, width // 8)
    received = lax.all_to_all(send, AXES, split_axis=0, concat_axis=0, tiled=True)
    part = vmem_call(
        expert_kernel, "experts", shape(received.shape, BF16), (received, w_gate, w_up, w_down), 1 << 32
    )
    back = lax.all_to_all(part, AXES, split_axis=0, concat_axis=0, tiled=True)
    out = vmem_call(
        combine_kernel, "combine", shape((n, width), BF16), (back, pick, gates, mixed), 1 << 30
    )
    return out.reshape(rows, cols, width)


def solution(mesh):
    placed = (
        P("lat", "lon", None),
        P(),
        P(),
        P(),
        P(),
        P("lat", "lon", None, None),
        P(None, ("lat", "lon")),
        P(None, ("lat", "lon")),
        P(("lat", "lon"), None),
    )
    return jax.shard_map(
        body, mesh=mesh, in_specs=placed, out_specs=P("lat", "lon", None), check_vma=False
    )
```

```python
import functools

import jax
import jax.numpy as jnp
from jax import lax
from jax.experimental import pallas as pl
from jax.experimental.pallas import tpu as pltpu
from jax.sharding import PartitionSpec as P

HEAD = 64
WIN = 8
MOST = 6
D = 1024
BLK = 256
BF16 = jnp.bfloat16
F32 = jnp.float32
AXES = ("lat", "lon")


def iota(shape, dim):
    return lax.broadcasted_iota(jnp.int32, shape, dim)


def dot(a, b):
    return jnp.dot(a, b, preferred_element_type=F32)


def rms(x):
    return x * lax.rsqrt(jnp.mean(x * x, axis=-1, keepdims=True) + 1e-05)


def head_norm(y):
    n = y.shape[1]
    same = jnp.where(iota((n, n), 0) // HEAD == iota((n, n), 1) // HEAD, 1.0, 0.0).astype(BF16)
    total = dot((y * y).astype(BF16), same)
    return (y * lax.rsqrt(total * (1.0 / HEAD) + 1e-05)).astype(BF16)


def vmem_call(kernel, name, out_shape, operands, flops, scratch=(), spaces=None):
    spaces = spaces or {}
    specs = [
        pl.BlockSpec(memory_space=spaces.get(i, pltpu.VMEM)) for i in range(len(operands))
    ]
    count = sum(a.size * a.dtype.itemsize for a in operands)
    outs = jax.tree.map(lambda _: pl.BlockSpec(memory_space=pltpu.VMEM), out_shape)
    return pl.pallas_call(
        kernel,
        in_specs=specs,
        out_specs=outs,
        out_shape=out_shape,
        scratch_shapes=list(scratch),
        compiler_params=pltpu.CompilerParams(vmem_limit_bytes=16 << 20),
        cost_estimate=pl.CostEstimate(flops=flops, bytes_accessed=count, transcendentals=0),
        name=name,
    )(*operands)


def contract_last(a, b):
    return lax.dot_general(a, b, (((1,), (1,)), ((), ())), preferred_element_type=F32)


def split_kernel(tokens_ref, x_ref, low_ref, high_ref):
    x = tokens_ref[...]
    x_ref[...] = x
    halves = x.astype(F32).reshape(-1, 2, WIN, D)
    low_ref[...] = halves[:, 0].reshape(-1, D).astype(BF16)
    high_ref[...] = halves[:, 1].reshape(-1, D).astype(BF16)


def plan_kernel(experts, shifts_ref, ids_ref, pack_ref, cells_ref, mask_ref, pick_ref):
    n = ids_ref.shape[1]
    shift_lat, shift_lon = shifts_ref[0], shifts_ref[1]
    cut_lat = WIN - shift_lat
    cut_lon = WIN - shift_lon
    expert = iota((experts, n), 0)
    hits = [ids_ref[k : k + 1, :] == expert for k in range(2)]
    both = jnp.where(hits[0] | hits[1], 1.0, 0.0)
    before = jnp.where(iota((n, n), 0) < iota((n, n), 1), 1.0, 0.0).astype(BF16)
    count = dot(both.astype(BF16), before)
    ranks = [jnp.sum(jnp.where(hit, count, 0.0), axis=0, keepdims=True) for hit in hits]
    ids = ids_ref[...].astype(F32)
    cell = iota((1, n), 1)
    flags = [
        jnp.where(flag, 1.0, 0.0)
        for flag in (cell >> 4 >= cut_lat, cell & 7 >= cut_lon, cell >> 3 >= cut_lat)
    ]
    lines = jnp.concatenate([ids, *ranks, *flags, jnp.zeros((1, n), F32)], axis=0)
    eye = jnp.where(iota((n, n), 0) == iota((n, n), 1), 1.0, 0.0).astype(BF16)
    cells = contract_last(eye, lines.astype(BF16))
    cells_ref[...] = cells
    slot = iota((MOST * experts, n), 0).astype(F32)
    codes = [ids[k : k + 1] * MOST + ranks[k] for k in range(2)]
    pack_ref[...] = jnp.where((slot == codes[0]) | (slot == codes[1]), 1.0, 0.0).astype(BF16)
    slot = iota((1, 2 * MOST * experts), 1)
    slot = (slot // (2 * MOST) * MOST + slot % MOST).astype(F32)
    for k in range(2):
        code = cells[:, k : k + 1] * MOST + cells[:, 2 + k : 3 + k]
        pick_ref[k * n : (k + 1) * n, :] = jnp.where(slot == code, 1.0, 0.0).astype(BF16)
    cell = iota((n, 1), 0)
    query = jnp.where(cell >> 4 >= cut_lat, 3, 0) + ((cell & 15) + shift_lon >> 3)
    key = iota((1, 3 * n), 1)
    narrow = key >= 2 * n
    halo_row = ((key >= n) & (key < 2 * n)) | (key >= 2 * n + WIN * WIN)
    past = jnp.where(narrow, key >> 3 & 7, key >> 4 & 7) >= cut_lat
    lat = lax.axis_index("lat")
    first, final = lat == 0, lat == lax.axis_size("lat") - 1
    beyond = halo_row & ((past & first) | (~past & final))
    window = jnp.where(past != halo_row, 3, 0) + jnp.where(
        narrow, jnp.where(key & 7 >= cut_lon, 0, 2), (key & 15) + shift_lon >> 3
    )
    valid = jnp.where(query == jnp.where(beyond, -1, window), 1.0, 0.0).astype(BF16)
    mask_ref[0:n, :] = valid
    mask_ref[n : 2 * n, :] = valid


def blocks(width):
    return [slice(i, i + width) for i in range(0, D, width)]


def keys_values(x, w_ref):
    keys = dot(x, w_ref[:, D : 2 * D]).astype(BF16).astype(F32)
    values = dot(x, w_ref[:, 2 * D :]).astype(BF16)
    return jnp.concatenate([head_norm(keys[:, lanes]) for lanes in blocks(BLK)], axis=1), values


def attend_keys(queries_ref, keys, values, mask):
    n = queries_ref.shape[0] // 2
    low_half = iota((1, 128), 1) < HEAD
    pairs = blocks(128)
    ones = jnp.ones((keys.shape[0], 128), BF16)
    scores = [contract_last(queries_ref[:, lanes], keys[:, lanes]) for lanes in pairs]
    weights = [jnp.exp(score).astype(BF16) * mask for score in scores]
    sums = [
        dot(weight, jnp.concatenate([values[:, lanes], ones], axis=1))
        for weight, lanes in zip(weights, pairs, strict=True)
    ]
    return [
        (
            jnp.where(low_half, both[0:n, 0:128], both[n:, 0:128]),
            jnp.where(low_half, both[0:n, 128:], both[n:, 128:]),
        )
        for both in sums
    ]


def own_kernel(x_ref, w_ref, qq_ref, k_ref, v_ref):
    n = x_ref.shape[0]
    x = rms(x_ref[...].astype(F32)).astype(BF16)
    queries = dot(x, w_ref[:, 0:D]).astype(BF16).astype(F32)
    k_ref[...], v_ref[...] = keys_values(x, w_ref)
    low_half = (iota((1, BLK), 1) & 127) < HEAD
    for lanes in blocks(BLK):
        q = head_norm(queries[:, lanes]).astype(F32) * 0.125
        qq_ref[0:n, lanes] = jnp.where(low_half, q, 0.0).astype(BF16)
        qq_ref[n:, lanes] = jnp.where(low_half, 0.0, q).astype(BF16)


def side_kernel(left_ref, right_ref, cells_ref, side_ref):
    n = side_ref.shape[0]
    side_ref[...] = jnp.where(
        cells_ref[0:n, 5:6] > 0.5, left_ref[...].astype(F32), right_ref[...].astype(F32)
    ).astype(BF16)


def near_kernel(
    up_ref, down_ref, side_ref, w_ref, mask_ref, cells_ref, qq_ref, k_ref, v_ref, num_ref, den_ref
):
    n = up_ref.shape[0]
    past = cells_ref[:, 4:5] > 0.5
    band = jnp.where(past, up_ref[...].astype(F32), down_ref[...].astype(F32))
    x = jnp.concatenate(
        [rms(band).astype(BF16), rms(side_ref[...].astype(F32)).astype(BF16)], axis=0
    )
    keys, values = keys_values(x, w_ref)
    keys = jnp.concatenate([k_ref[...], keys], axis=0)
    values = jnp.concatenate([v_ref[...], values], axis=0)
    sums = attend_keys(qq_ref, keys, values, mask_ref[:, 0 : keys.shape[0]])
    for lanes, (num, den) in zip(blocks(128), sums, strict=True):
        num_ref[:, lanes] = num
        den_ref[:, lanes] = den


def last_kernel(
    x_ref, up_ref, down_ref, w_ref, mask_ref, qq_ref, num_ref, den_ref,
    wo_ref, router_ref, cells_ref, pack_ref, mixed_ref, gates_ref, send_ref,
):
    n = x_ref.shape[0]
    m = up_ref.shape[0]
    past = cells_ref[0:m, 6:7] > 0.5
    corner = jnp.where(past, up_ref[...].astype(F32), down_ref[...].astype(F32))
    keys, values = keys_values(rms(corner).astype(BF16), w_ref)
    sums = attend_keys(qq_ref, keys, values, mask_ref[:, 3 * n - m :])
    attended = [
        ((num_ref[:, lanes] + num) / (den_ref[:, lanes] + den)).astype(BF16)
        for lanes, (num, den) in zip(blocks(128), sums, strict=True)
    ]
    total = dot(jnp.concatenate(attended, axis=1), wo_ref[...])
    mixed = (x_ref[...].astype(F32) + total).astype(BF16)
    mixed_ref[...] = mixed
    normed = rms(mixed.astype(F32)).astype(BF16)
    logits = contract_last(normed, router_ref[...])
    experts = logits.shape[1]
    expert = iota(logits.shape, 1).astype(F32)
    sig = [
        jax.nn.sigmoid(
            jnp.sum(jnp.where(cells_ref[:, k : k + 1] == expert, logits, 0.0), axis=1, keepdims=True)
        )
        for k in range(2)
    ]
    gates_ref[...] = jnp.where(iota((n, 128), 1) == 0, sig[0], sig[1]) / (sig[0] + sig[1])
    rows = dot(pack_ref[...], normed).astype(BF16).reshape(-1, 8, 128)
    rows = rows.reshape(experts, MOST, 8, 128)
    send_ref[:, 0] = rows
    send_ref[:, 1] = rows


def expert_kernel(rows_ref, wg_ref, wu_ref, wd_ref, out_ref):
    x = rows_ref[...].reshape(-1, D)
    gate = dot(x, wg_ref[...])
    upper = dot(x, wu_ref[...])
    hidden = (jax.nn.silu(gate) * upper).astype(BF16)
    out_ref[...] = dot(hidden, wd_ref[...]).astype(BF16).reshape(out_ref.shape)


def combine_kernel(back_ref, pick_ref, gates_ref, mixed_ref, out_ref):
    n = mixed_ref.shape[0]
    both = dot(pick_ref[...], back_ref[...].reshape(-1, D))
    moe = gates_ref[:, 0:1] * both[0:n] + gates_ref[:, 1:2] * both[n:]
    out_ref[...] = (mixed_ref[...].astype(F32) + moe).astype(BF16)


def moved(x, down, right):
    n_lat, n_lon = lax.axis_size("lat"), lax.axis_size("lon")
    pairs = [
        (i * n_lon + j, (i + down) % n_lat * n_lon + (j + right) % n_lon)
        for i in range(n_lat)
        for j in range(n_lon)
    ]
    return lax.ppermute(x, AXES, pairs)


def body(tokens, shifts, w_qkv, w_out, router, expert_ids, w_gate, w_up, w_down):
    rows, cols, width = tokens.shape
    n = rows * cols
    experts = router.shape[1]
    shape = jax.ShapeDtypeStruct
    half = shape((n // 2, width), BF16)
    x, low, high = vmem_call(
        split_kernel,
        "split",
        [shape((n, width), BF16), half, half],
        (tokens.reshape(n, width),),
        3 << 30,
    )
    up = moved(x, 1, 0)
    down = moved(x, -1, 0)
    left = moved(high, 0, 1)
    right = moved(low, 0, -1)
    whole = shape((n, width), BF16)
    qq, keys, values = vmem_call(
        own_kernel,
        "own",
        [shape((2 * n, width), BF16), whole, whole],
        (x, w_qkv),
        6 * n * width * width,
    )
    shifts, ids, keys = lax.optimization_barrier((shifts, expert_ids.reshape(n, 2).T, keys))
    pack, cells, mask, pick = vmem_call(
        functools.partial(plan_kernel, experts),
        "plan",
        [
            shape((MOST * experts, n), BF16),
            shape((n, 8), F32),
            shape((2 * n, 3 * n), BF16),
            shape((2 * n, 2 * MOST * experts), BF16),
        ],
        (shifts, ids),
        1 << 30,
        spaces={0: pltpu.SMEM},
    )
    side = vmem_call(side_kernel, "side", half, (left, right, cells), 1 << 10)
    up_side = moved(side, 1, 0)
    down_side = moved(side, -1, 0)
    num, den = vmem_call(
        near_kernel,
        "near",
        [shape((n, width), F32)] * 2,
        (up, down, side, w_qkv, mask, cells, qq, keys, values),
        8 * n * width * width,
    )
    mixed, gates, send = vmem_call(
        last_kernel,
        "last",
        [
            shape((n, width), BF16),
            shape((n, 128), F32),
            shape((experts, 2, MOST, 8, width // 8), BF16),
        ],
        (x, up_side, down_side, w_qkv, mask, qq, num, den, w_out, router.T, cells, pack),
        6 * n * width * width,
    )
    send = send.reshape(2 * experts * MOST, 8, width // 8)
    received = lax.all_to_all(send, AXES, split_axis=0, concat_axis=0, tiled=True)
    part = vmem_call(
        expert_kernel, "experts", shape(received.shape, BF16), (received, w_gate, w_up, w_down), 1 << 32
    )
    back = lax.all_to_all(part, AXES, split_axis=0, concat_axis=0, tiled=True)
    out = vmem_call(
        combine_kernel, "combine", shape((n, width), BF16), (back, pick, gates, mixed), 1 << 30
    )
    return out.reshape(rows, cols, width)


def solution(mesh):
    placed = (
        P("lat", "lon", None),
        P(),
        P(),
        P(),
        P(),
        P("lat", "lon", None, None),
        P(None, ("lat", "lon")),
        P(None, ("lat", "lon")),
        P(("lat", "lon"), None),
    )
    return jax.shard_map(
        body, mesh=mesh, in_specs=placed, out_specs=P("lat", "lon", None), check_vma=False
    )
```

```python
import functools

import jax
import jax.numpy as jnp
from jax import lax
from jax.experimental import pallas as pl
from jax.experimental.pallas import tpu as pltpu
from jax.sharding import PartitionSpec as P

HEAD = 64
WIN = 8
MOST = 6
D = 1024
BLK = 256
BF16 = jnp.bfloat16
F32 = jnp.float32
AXES = ("lat", "lon")


def iota(shape, dim):
    return lax.broadcasted_iota(jnp.int32, shape, dim)


def dot(a, b):
    return jnp.dot(a, b, preferred_element_type=F32)


def rms(x):
    return x * lax.rsqrt(jnp.mean(x * x, axis=-1, keepdims=True) + 1e-05)


def head_norm(y):
    n = y.shape[1]
    same = jnp.where(iota((n, n), 0) // HEAD == iota((n, n), 1) // HEAD, 1.0, 0.0).astype(BF16)
    total = dot((y * y).astype(BF16), same)
    return (y * lax.rsqrt(total * (1.0 / HEAD) + 1e-05)).astype(BF16)


def vmem_call(kernel, name, out_shape, operands, flops, scratch=(), spaces=None):
    spaces = spaces or {}
    specs = [
        pl.BlockSpec(memory_space=spaces.get(i, pltpu.VMEM)) for i in range(len(operands))
    ]
    count = sum(a.size * a.dtype.itemsize for a in operands)
    outs = jax.tree.map(lambda _: pl.BlockSpec(memory_space=pltpu.VMEM), out_shape)
    return pl.pallas_call(
        kernel,
        in_specs=specs,
        out_specs=outs,
        out_shape=out_shape,
        scratch_shapes=list(scratch),
        compiler_params=pltpu.CompilerParams(vmem_limit_bytes=16 << 20),
        cost_estimate=pl.CostEstimate(flops=flops, bytes_accessed=count, transcendentals=0),
        name=name,
    )(*operands)


def contract_last(a, b):
    return lax.dot_general(a, b, (((1,), (1,)), ((), ())), preferred_element_type=F32)


def split_kernel(tokens_ref, x_ref, low_ref, high_ref, up_ref, down_ref):
    x = tokens_ref[...]
    x_ref[...] = x
    up_ref[...] = x
    down_ref[...] = x
    halves = x.astype(F32).reshape(-1, 2, WIN, D)
    low_ref[...] = halves[:, 0].reshape(-1, D).astype(BF16)
    high_ref[...] = halves[:, 1].reshape(-1, D).astype(BF16)


def plan_kernel(experts, shifts_ref, ids_ref, pack_ref, cells_ref, mask_ref, pick_ref):
    n = ids_ref.shape[1]
    shift_lat, shift_lon = shifts_ref[0], shifts_ref[1]
    cut_lat = WIN - shift_lat
    cut_lon = WIN - shift_lon
    expert = iota((experts, n), 0)
    hits = [ids_ref[k : k + 1, :] == expert for k in range(2)]
    both = jnp.where(hits[0] | hits[1], 1.0, 0.0)
    before = jnp.where(iota((n, n), 0) < iota((n, n), 1), 1.0, 0.0).astype(BF16)
    count = dot(both.astype(BF16), before)
    ranks = [jnp.sum(jnp.where(hit, count, 0.0), axis=0, keepdims=True) for hit in hits]
    ids = ids_ref[...].astype(F32)
    cell = iota((1, n), 1)
    flags = [
        jnp.where(flag, 1.0, 0.0)
        for flag in (cell >> 4 >= cut_lat, cell & 7 >= cut_lon, cell >> 3 >= cut_lat)
    ]
    lines = jnp.concatenate([ids, *ranks, *flags, jnp.zeros((1, n), F32)], axis=0)
    eye = jnp.where(iota((n, n), 0) == iota((n, n), 1), 1.0, 0.0).astype(BF16)
    cells = contract_last(eye, lines.astype(BF16))
    cells_ref[...] = cells
    slot = iota((MOST * experts, n), 0).astype(F32)
    codes = [ids[k : k + 1] * MOST + ranks[k] for k in range(2)]
    pack_ref[...] = jnp.where((slot == codes[0]) | (slot == codes[1]), 1.0, 0.0).astype(BF16)
    slot = iota((1, 2 * MOST * experts), 1)
    slot = (slot // (2 * MOST) * MOST + slot % MOST).astype(F32)
    for k in range(2):
        code = cells[:, k : k + 1] * MOST + cells[:, 2 + k : 3 + k]
        pick_ref[k * n : (k + 1) * n, :] = jnp.where(slot == code, 1.0, 0.0).astype(BF16)
    cell = iota((n, 1), 0)
    query = jnp.where(cell >> 4 >= cut_lat, 3, 0) + ((cell & 15) + shift_lon >> 3)
    key = iota((1, 3 * n), 1)
    narrow = key >= 2 * n
    halo_row = ((key >= n) & (key < 2 * n)) | (key >= 2 * n + WIN * WIN)
    past = jnp.where(narrow, key >> 3 & 7, key >> 4 & 7) >= cut_lat
    lat = lax.axis_index("lat")
    first, final = lat == 0, lat == lax.axis_size("lat") - 1
    beyond = halo_row & ((past & first) | (~past & final))
    window = jnp.where(past != halo_row, 3, 0) + jnp.where(
        narrow, jnp.where(key & 7 >= cut_lon, 0, 2), (key & 15) + shift_lon >> 3
    )
    valid = jnp.where(query == jnp.where(beyond, -1, window), 1.0, 0.0).astype(BF16)
    mask_ref[0:n, :] = valid
    mask_ref[n : 2 * n, :] = valid


def blocks(width):
    return [slice(i, i + width) for i in range(0, D, width)]


def keys_values(x, w_ref):
    keys = dot(x, w_ref[:, D : 2 * D]).astype(BF16).astype(F32)
    values = dot(x, w_ref[:, 2 * D :]).astype(BF16)
    return jnp.concatenate([head_norm(keys[:, lanes]) for lanes in blocks(BLK)], axis=1), values


def attend_keys(queries_ref, keys, values, mask):
    n = queries_ref.shape[0] // 2
    low_half = iota((1, 128), 1) < HEAD
    pairs = blocks(128)
    ones = jnp.ones((keys.shape[0], 128), BF16)
    scores = [contract_last(queries_ref[:, lanes], keys[:, lanes]) for lanes in pairs]
    weights = [jnp.exp(score).astype(BF16) * mask for score in scores]
    sums = [
        dot(weight, jnp.concatenate([values[:, lanes], ones], axis=1))
        for weight, lanes in zip(weights, pairs, strict=True)
    ]
    return [
        (
            jnp.where(low_half, both[0:n, 0:128], both[n:, 0:128]),
            jnp.where(low_half, both[0:n, 128:], both[n:, 128:]),
        )
        for both in sums
    ]


def own_kernel(x_ref, w_ref, qq_ref, k_ref, v_ref):
    n = x_ref.shape[0]
    x = rms(x_ref[...].astype(F32)).astype(BF16)
    queries = dot(x, w_ref[:, 0:D]).astype(BF16).astype(F32)
    k_ref[...], v_ref[...] = keys_values(x, w_ref)
    low_half = (iota((1, BLK), 1) & 127) < HEAD
    for lanes in blocks(BLK):
        q = head_norm(queries[:, lanes]).astype(F32) * 0.125
        qq_ref[0:n, lanes] = jnp.where(low_half, q, 0.0).astype(BF16)
        qq_ref[n:, lanes] = jnp.where(low_half, 0.0, q).astype(BF16)


def side_kernel(left_ref, right_ref, cells_ref, side_ref):
    n = side_ref.shape[0]
    side_ref[...] = jnp.where(
        cells_ref[0:n, 5:6] > 0.5, left_ref[...].astype(F32), right_ref[...].astype(F32)
    ).astype(BF16)


def near_kernel(
    up_ref, down_ref, side_ref, w_ref, mask_ref, cells_ref, qq_ref, k_ref, v_ref, num_ref, den_ref
):
    n = up_ref.shape[0]
    past = cells_ref[:, 4:5] > 0.5
    band = jnp.where(past, up_ref[...].astype(F32), down_ref[...].astype(F32))
    x = jnp.concatenate(
        [rms(band).astype(BF16), rms(side_ref[...].astype(F32)).astype(BF16)], axis=0
    )
    keys, values = keys_values(x, w_ref)
    keys = jnp.concatenate([k_ref[...], keys], axis=0)
    values = jnp.concatenate([v_ref[...], values], axis=0)
    sums = attend_keys(qq_ref, keys, values, mask_ref[:, 0 : keys.shape[0]])
    for lanes, (num, den) in zip(blocks(128), sums, strict=True):
        num_ref[:, lanes] = num
        den_ref[:, lanes] = den


def last_kernel(
    x_ref, up_ref, down_ref, w_ref, mask_ref, qq_ref, num_ref, den_ref,
    wo_ref, router_ref, cells_ref, pack_ref, mixed_ref, gates_ref, send_ref,
):
    n = x_ref.shape[0]
    m = up_ref.shape[0]
    past = cells_ref[0:m, 6:7] > 0.5
    corner = jnp.where(past, up_ref[...].astype(F32), down_ref[...].astype(F32))
    keys, values = keys_values(rms(corner).astype(BF16), w_ref)
    sums = attend_keys(qq_ref, keys, values, mask_ref[:, 3 * n - m :])
    attended = [
        ((num_ref[:, lanes] + num) / (den_ref[:, lanes] + den)).astype(BF16)
        for lanes, (num, den) in zip(blocks(128), sums, strict=True)
    ]
    total = dot(jnp.concatenate(attended, axis=1), wo_ref[...])
    mixed = (x_ref[...].astype(F32) + total).astype(BF16)
    mixed_ref[...] = mixed
    normed = rms(mixed.astype(F32)).astype(BF16)
    logits = contract_last(normed, router_ref[...])
    experts = logits.shape[1]
    expert = iota(logits.shape, 1).astype(F32)
    sig = [
        jax.nn.sigmoid(
            jnp.sum(jnp.where(cells_ref[:, k : k + 1] == expert, logits, 0.0), axis=1, keepdims=True)
        )
        for k in range(2)
    ]
    gates_ref[...] = jnp.where(iota((n, 128), 1) == 0, sig[0], sig[1]) / (sig[0] + sig[1])
    rows = dot(pack_ref[...], normed).astype(BF16).reshape(-1, 8, 128)
    rows = rows.reshape(experts, MOST, 8, 128)
    send_ref[:, 0] = rows
    send_ref[:, 1] = rows


def expert_kernel(rows_ref, wg_ref, wu_ref, wd_ref, out_ref):
    x = rows_ref[...].reshape(-1, D)
    gate = dot(x, wg_ref[...])
    upper = dot(x, wu_ref[...])
    hidden = (jax.nn.silu(gate) * upper).astype(BF16)
    out_ref[...] = dot(hidden, wd_ref[...]).astype(BF16).reshape(out_ref.shape)


def combine_kernel(back_ref, pick_ref, gates_ref, mixed_ref, out_ref):
    n = mixed_ref.shape[0]
    both = dot(pick_ref[...], back_ref[...].reshape(-1, D))
    moe = gates_ref[:, 0:1] * both[0:n] + gates_ref[:, 1:2] * both[n:]
    out_ref[...] = (mixed_ref[...].astype(F32) + moe).astype(BF16)


def moved(x, down, right):
    n_lat, n_lon = lax.axis_size("lat"), lax.axis_size("lon")
    pairs = [
        (i * n_lon + j, (i + down) % n_lat * n_lon + (j + right) % n_lon)
        for i in range(n_lat)
        for j in range(n_lon)
    ]
    return lax.ppermute(x, AXES, pairs)


def body(tokens, shifts, w_qkv, w_out, router, expert_ids, w_gate, w_up, w_down):
    rows, cols, width = tokens.shape
    n = rows * cols
    experts = router.shape[1]
    shape = jax.ShapeDtypeStruct
    half = shape((n // 2, width), BF16)
    x, low, high, for_up, for_down = vmem_call(
        split_kernel,
        "split",
        [shape((n, width), BF16), half, half, *[shape((n, width), BF16)] * 2],
        (tokens.reshape(n, width),),
        3 << 30,
    )
    up = moved(for_up, 1, 0)
    down = moved(for_down, -1, 0)
    left = moved(high, 0, 1)
    right = moved(low, 0, -1)
    whole = shape((n, width), BF16)
    qq, keys, values = vmem_call(
        own_kernel,
        "own",
        [shape((2 * n, width), BF16), whole, whole],
        (x, w_qkv),
        6 * n * width * width,
    )
    shifts, ids, keys = lax.optimization_barrier((shifts, expert_ids.reshape(n, 2).T, keys))
    pack, cells, mask, pick = vmem_call(
        functools.partial(plan_kernel, experts),
        "plan",
        [
            shape((MOST * experts, n), BF16),
            shape((n, 8), F32),
            shape((2 * n, 3 * n), BF16),
            shape((2 * n, 2 * MOST * experts), BF16),
        ],
        (shifts, ids),
        1 << 30,
        spaces={0: pltpu.SMEM},
    )
    side = vmem_call(side_kernel, "side", half, (left, right, cells), 1 << 10)
    up_side = moved(side, 1, 0)
    down_side = moved(side, -1, 0)
    num, den = vmem_call(
        near_kernel,
        "near",
        [shape((n, width), F32)] * 2,
        (up, down, side, w_qkv, mask, cells, qq, keys, values),
        8 * n * width * width,
    )
    mixed, gates, send = vmem_call(
        last_kernel,
        "last",
        [
            shape((n, width), BF16),
            shape((n, 128), F32),
            shape((experts, 2, MOST, 8, width // 8), BF16),
        ],
        (x, up_side, down_side, w_qkv, mask, qq, num, den, w_out, router.T, cells, pack),
        6 * n * width * width,
    )
    send = send.reshape(2 * experts * MOST, 8, width // 8)
    received = lax.all_to_all(send, AXES, split_axis=0, concat_axis=0, tiled=True)
    part = vmem_call(
        expert_kernel, "experts", shape(received.shape, BF16), (received, w_gate, w_up, w_down), 1 << 32
    )
    back = lax.all_to_all(part, AXES, split_axis=0, concat_axis=0, tiled=True)
    out = vmem_call(
        combine_kernel, "combine", shape((n, width), BF16), (back, pick, gates, mixed), 1 << 30
    )
    return out.reshape(rows, cols, width)


def solution(mesh):
    placed = (
        P("lat", "lon", None),
        P(),
        P(),
        P(),
        P(),
        P("lat", "lon", None, None),
        P(None, ("lat", "lon")),
        P(None, ("lat", "lon")),
        P(("lat", "lon"), None),
    )
    return jax.shard_map(
        body, mesh=mesh, in_specs=placed, out_specs=P("lat", "lon", None), check_vma=False
    )
```

```python
import functools

import jax
import jax.numpy as jnp
from jax import lax
from jax.experimental import pallas as pl
from jax.experimental.pallas import tpu as pltpu
from jax.sharding import PartitionSpec as P

HEAD = 64
WIN = 8
MOST = 6
D = 1024
BLK = 256
BF16 = jnp.bfloat16
F32 = jnp.float32
AXES = ("lat", "lon")


def iota(shape, dim):
    return lax.broadcasted_iota(jnp.int32, shape, dim)


def dot(a, b):
    return jnp.dot(a, b, preferred_element_type=F32)


def rms(x):
    return x * lax.rsqrt(jnp.mean(x * x, axis=-1, keepdims=True) + 1e-05)


def head_norm(y):
    n = y.shape[1]
    same = jnp.where(iota((n, n), 0) // HEAD == iota((n, n), 1) // HEAD, 1.0, 0.0).astype(BF16)
    total = dot((y * y).astype(BF16), same)
    return (y * lax.rsqrt(total * (1.0 / HEAD) + 1e-05)).astype(BF16)


def vmem_call(kernel, name, out_shape, operands, flops, scratch=(), spaces=None):
    spaces = spaces or {}
    specs = [
        pl.BlockSpec(memory_space=spaces.get(i, pltpu.VMEM)) for i in range(len(operands))
    ]
    count = sum(a.size * a.dtype.itemsize for a in operands)
    outs = jax.tree.map(lambda _: pl.BlockSpec(memory_space=pltpu.VMEM), out_shape)
    return pl.pallas_call(
        kernel,
        in_specs=specs,
        out_specs=outs,
        out_shape=out_shape,
        scratch_shapes=list(scratch),
        compiler_params=pltpu.CompilerParams(vmem_limit_bytes=16 << 20),
        cost_estimate=pl.CostEstimate(flops=flops, bytes_accessed=count, transcendentals=0),
        name=name,
    )(*operands)


def contract_last(a, b):
    return lax.dot_general(a, b, (((1,), (1,)), ((), ())), preferred_element_type=F32)


def split_kernel(tokens_ref, x_ref, low_ref, high_ref, down_ref):
    x = tokens_ref[...]
    x_ref[...] = x
    down_ref[...] = x
    halves = x.astype(F32).reshape(-1, 2, WIN, D)
    low_ref[...] = halves[:, 0].reshape(-1, D).astype(BF16)
    high_ref[...] = halves[:, 1].reshape(-1, D).astype(BF16)


def plan_kernel(experts, shifts_ref, ids_ref, pack_ref, cells_ref, mask_ref, pick_ref):
    n = ids_ref.shape[1]
    shift_lat, shift_lon = shifts_ref[0], shifts_ref[1]
    cut_lat = WIN - shift_lat
    cut_lon = WIN - shift_lon
    expert = iota((experts, n), 0)
    hits = [ids_ref[k : k + 1, :] == expert for k in range(2)]
    both = jnp.where(hits[0] | hits[1], 1.0, 0.0)
    before = jnp.where(iota((n, n), 0) < iota((n, n), 1), 1.0, 0.0).astype(BF16)
    count = dot(both.astype(BF16), before)
    ranks = [jnp.sum(jnp.where(hit, count, 0.0), axis=0, keepdims=True) for hit in hits]
    ids = ids_ref[...].astype(F32)
    cell = iota((1, n), 1)
    flags = [
        jnp.where(flag, 1.0, 0.0)
        for flag in (cell >> 4 >= cut_lat, cell & 7 >= cut_lon, cell >> 3 >= cut_lat)
    ]
    lines = jnp.concatenate([ids, *ranks, *flags, jnp.zeros((1, n), F32)], axis=0)
    eye = jnp.where(iota((n, n), 0) == iota((n, n), 1), 1.0, 0.0).astype(BF16)
    cells = contract_last(eye, lines.astype(BF16))
    cells_ref[...] = cells
    slot = iota((MOST * experts, n), 0).astype(F32)
    codes = [ids[k : k + 1] * MOST + ranks[k] for k in range(2)]
    pack_ref[...] = jnp.where((slot == codes[0]) | (slot == codes[1]), 1.0, 0.0).astype(BF16)
    slot = iota((1, 2 * MOST * experts), 1)
    slot = (slot // (2 * MOST) * MOST + slot % MOST).astype(F32)
    for k in range(2):
        code = cells[:, k : k + 1] * MOST + cells[:, 2 + k : 3 + k]
        pick_ref[k * n : (k + 1) * n, :] = jnp.where(slot == code, 1.0, 0.0).astype(BF16)
    cell = iota((n, 1), 0)
    query = jnp.where(cell >> 4 >= cut_lat, 3, 0) + ((cell & 15) + shift_lon >> 3)
    key = iota((1, 3 * n), 1)
    narrow = key >= 2 * n
    halo_row = ((key >= n) & (key < 2 * n)) | (key >= 2 * n + WIN * WIN)
    past = jnp.where(narrow, key >> 3 & 7, key >> 4 & 7) >= cut_lat
    lat = lax.axis_index("lat")
    first, final = lat == 0, lat == lax.axis_size("lat") - 1
    beyond = halo_row & ((past & first) | (~past & final))
    window = jnp.where(past != halo_row, 3, 0) + jnp.where(
        narrow, jnp.where(key & 7 >= cut_lon, 0, 2), (key & 15) + shift_lon >> 3
    )
    valid = jnp.where(query == jnp.where(beyond, -1, window), 1.0, 0.0).astype(BF16)
    mask_ref[0:n, :] = valid
    mask_ref[n : 2 * n, :] = valid


def blocks(width):
    return [slice(i, i + width) for i in range(0, D, width)]


def keys_values(x, w_ref):
    keys = dot(x, w_ref[:, D : 2 * D]).astype(BF16).astype(F32)
    values = dot(x, w_ref[:, 2 * D :]).astype(BF16)
    return jnp.concatenate([head_norm(keys[:, lanes]) for lanes in blocks(BLK)], axis=1), values


def attend_keys(queries_ref, keys, values, mask, scale=None):
    n = queries_ref.shape[0] // 2
    low_half = iota((1, 128), 1) < HEAD
    pairs = blocks(128)
    ones = jnp.ones((keys.shape[0], 128), BF16)
    scores = [contract_last(queries_ref[:, lanes], keys[:, lanes]) for lanes in pairs]
    if scale is not None:
        scores = [
            jnp.concatenate(
                [score[0:n] * scale[2 * i : 2 * i + 1], score[n:] * scale[2 * i + 1 : 2 * i + 2]], axis=0
            )
            for i, score in enumerate(scores)
        ]
    weights = [jnp.exp(score).astype(BF16) * mask for score in scores]
    sums = [
        dot(weight, jnp.concatenate([values[:, lanes], ones], axis=1))
        for weight, lanes in zip(weights, pairs, strict=True)
    ]
    return [
        (
            jnp.where(low_half, both[0:n, 0:128], both[n:, 0:128]),
            jnp.where(low_half, both[0:n, 128:], both[n:, 128:]),
        )
        for both in sums
    ]


def own_kernel(x_ref, w_ref, qq_ref, k_ref, v_ref):
    n = x_ref.shape[0]
    x = rms(x_ref[...].astype(F32)).astype(BF16)
    queries = dot(x, w_ref[:, 0:D]).astype(BF16).astype(F32)
    k_ref[...], v_ref[...] = keys_values(x, w_ref)
    low_half = (iota((1, BLK), 1) & 127) < HEAD
    for lanes in blocks(BLK):
        q = head_norm(queries[:, lanes]).astype(F32) * 0.125
        qq_ref[0:n, lanes] = jnp.where(low_half, q, 0.0).astype(BF16)
        qq_ref[n:, lanes] = jnp.where(low_half, 0.0, q).astype(BF16)


def side_kernel(left_ref, right_ref, cells_ref, side_ref):
    n = side_ref.shape[0]
    side_ref[...] = jnp.where(
        cells_ref[0:n, 5:6] > 0.5, left_ref[...].astype(F32), right_ref[...].astype(F32)
    ).astype(BF16)


def near_kernel(
    up_ref, down_ref, side_ref, w_ref, mask_ref, cells_ref, qq_ref, k_ref, v_ref, num_ref, den_ref
):
    n = up_ref.shape[0]
    past = cells_ref[:, 4:5] > 0.5
    band = jnp.where(past, up_ref[...].astype(F32), down_ref[...].astype(F32))
    x = jnp.concatenate(
        [rms(band).astype(BF16), rms(side_ref[...].astype(F32)).astype(BF16)], axis=0
    )
    keys, values = keys_values(x, w_ref)
    keys = jnp.concatenate([k_ref[...], keys], axis=0)
    values = jnp.concatenate([v_ref[...], values], axis=0)
    sums = attend_keys(qq_ref, keys, values, mask_ref[:, 0 : keys.shape[0]])
    for lanes, (num, den) in zip(blocks(128), sums, strict=True):
        num_ref[:, lanes] = num
        den_ref[:, lanes] = den


def last_kernel(
    x_ref, up_ref, down_ref, w_ref, mask_ref, qq_ref, num_ref, den_ref,
    wo_ref, router_ref, cells_ref, pack_ref, mixed_ref, gates_ref, send_ref,
):
    n = x_ref.shape[0]
    m = up_ref.shape[0]
    past = cells_ref[0:m, 6:7] > 0.5
    corner = jnp.where(past, up_ref[...].astype(F32), down_ref[...].astype(F32))
    x = rms(corner).astype(BF16)
    keys = dot(x, w_ref[:, D : 2 * D]).astype(BF16)
    values = dot(x, w_ref[:, 2 * D :]).astype(BF16)
    heads = D // HEAD
    head = jnp.where(iota((heads, D), 0) == iota((heads, D), 1) // HEAD, 1.0, 0.0).astype(BF16)
    square = keys.astype(F32) * keys.astype(F32)
    scale = lax.rsqrt(contract_last(head, square.astype(BF16)) * (1.0 / HEAD) + 1e-05)
    sums = attend_keys(qq_ref, keys, values, mask_ref[:, 3 * n - m :], scale)
    attended = [
        ((num_ref[:, lanes] + num) / (den_ref[:, lanes] + den)).astype(BF16)
        for lanes, (num, den) in zip(blocks(128), sums, strict=True)
    ]
    total = dot(jnp.concatenate(attended, axis=1), wo_ref[...])
    mixed = (x_ref[...].astype(F32) + total).astype(BF16)
    mixed_ref[...] = mixed
    normed = rms(mixed.astype(F32)).astype(BF16)
    logits = contract_last(normed, router_ref[...])
    experts = logits.shape[1]
    expert = iota(logits.shape, 1).astype(F32)
    sig = [
        jax.nn.sigmoid(
            jnp.sum(jnp.where(cells_ref[:, k : k + 1] == expert, logits, 0.0), axis=1, keepdims=True)
        )
        for k in range(2)
    ]
    gates_ref[...] = jnp.where(iota((n, 128), 1) == 0, sig[0], sig[1]) / (sig[0] + sig[1])
    rows = dot(pack_ref[...], normed).astype(BF16).reshape(-1, 8, 128)
    rows = rows.reshape(experts, MOST, 8, 128)
    send_ref[:, 0] = rows
    send_ref[:, 1] = rows


def expert_kernel(rows_ref, wg_ref, wu_ref, wd_ref, out_ref):
    x = rows_ref[...].reshape(-1, D)
    gate = dot(x, wg_ref[...])
    upper = dot(x, wu_ref[...])
    hidden = (jax.nn.silu(gate) * upper).astype(BF16)
    out_ref[...] = dot(hidden, wd_ref[...]).astype(BF16).reshape(out_ref.shape)


def combine_kernel(back_ref, pick_ref, gates_ref, mixed_ref, out_ref):
    n = mixed_ref.shape[0]
    both = dot(pick_ref[...], back_ref[...].reshape(-1, D))
    moe = gates_ref[:, 0:1] * both[0:n] + gates_ref[:, 1:2] * both[n:]
    out_ref[...] = (mixed_ref[...].astype(F32) + moe).astype(BF16)


def moved(x, down, right):
    n_lat, n_lon = lax.axis_size("lat"), lax.axis_size("lon")
    pairs = [
        (i * n_lon + j, (i + down) % n_lat * n_lon + (j + right) % n_lon)
        for i in range(n_lat)
        for j in range(n_lon)
    ]
    return lax.ppermute(x, AXES, pairs)


def body(tokens, shifts, w_qkv, w_out, router, expert_ids, w_gate, w_up, w_down):
    rows, cols, width = tokens.shape
    n = rows * cols
    experts = router.shape[1]
    shape = jax.ShapeDtypeStruct
    half = shape((n // 2, width), BF16)
    x, low, high, for_down = vmem_call(
        split_kernel,
        "split",
        [shape((n, width), BF16), half, half, shape((n, width), BF16)],
        (tokens.reshape(n, width),),
        3 << 30,
    )
    left = moved(high, 0, 1)
    right = moved(low, 0, -1)
    later, _, _ = lax.optimization_barrier((tokens.reshape(n, width), high, low))
    up = moved(later, 1, 0)
    down = moved(for_down, -1, 0)
    whole = shape((n, width), BF16)
    qq, keys, values = vmem_call(
        own_kernel,
        "own",
        [shape((2 * n, width), BF16), whole, whole],
        (x, w_qkv),
        6 * n * width * width,
    )
    shifts, ids, keys = lax.optimization_barrier((shifts, expert_ids.reshape(n, 2).T, keys))
    pack, cells, mask, pick = vmem_call(
        functools.partial(plan_kernel, experts),
        "plan",
        [
            shape((MOST * experts, n), BF16),
            shape((n, 8), F32),
            shape((2 * n, 3 * n), BF16),
            shape((2 * n, 2 * MOST * experts), BF16),
        ],
        (shifts, ids),
        1 << 30,
        spaces={0: pltpu.SMEM},
    )
    side = vmem_call(side_kernel, "side", half, (left, right, cells), 1 << 10)
    up_side = moved(side, 1, 0)
    down_side = moved(side, -1, 0)
    num, den = vmem_call(
        near_kernel,
        "near",
        [shape((n, width), F32)] * 2,
        (up, down, side, w_qkv, mask, cells, qq, keys, values),
        8 * n * width * width,
    )
    mixed, gates, send = vmem_call(
        last_kernel,
        "last",
        [
            shape((n, width), BF16),
            shape((n, 128), F32),
            shape((experts, 2, MOST, 8, width // 8), BF16),
        ],
        (x, up_side, down_side, w_qkv, mask, qq, num, den, w_out, router.T, cells, pack),
        6 * n * width * width,
    )
    send = send.reshape(2 * experts * MOST, 8, width // 8)
    received = lax.all_to_all(send, AXES, split_axis=0, concat_axis=0, tiled=True)
    part = vmem_call(
        expert_kernel, "experts", shape(received.shape, BF16), (received, w_gate, w_up, w_down), 1 << 32
    )
    back = lax.all_to_all(part, AXES, split_axis=0, concat_axis=0, tiled=True)
    out = vmem_call(
        combine_kernel, "combine", shape((n, width), BF16), (back, pick, gates, mixed), 1 << 30
    )
    return out.reshape(rows, cols, width)


def solution(mesh):
    placed = (
        P("lat", "lon", None),
        P(),
        P(),
        P(),
        P(),
        P("lat", "lon", None, None),
        P(None, ("lat", "lon")),
        P(None, ("lat", "lon")),
        P(("lat", "lon"), None),
    )
    return jax.shard_map(
        body, mesh=mesh, in_specs=placed, out_specs=P("lat", "lon", None), check_vma=False
    )
```

```python
import functools

import jax
import jax.numpy as jnp
from jax import lax
from jax.experimental import pallas as pl
from jax.experimental.pallas import tpu as pltpu
from jax.sharding import PartitionSpec as P

HEAD = 64
WIN = 8
MOST = 6
D = 1024
BLK = 256
BF16 = jnp.bfloat16
F32 = jnp.float32
AXES = ("lat", "lon")


def iota(shape, dim):
    return lax.broadcasted_iota(jnp.int32, shape, dim)


def dot(a, b):
    return jnp.dot(a, b, preferred_element_type=F32)


def rms(x):
    return x * lax.rsqrt(jnp.mean(x * x, axis=-1, keepdims=True) + 1e-05)


def head_norm(y):
    n = y.shape[1]
    same = jnp.where(iota((n, n), 0) // HEAD == iota((n, n), 1) // HEAD, 1.0, 0.0).astype(BF16)
    total = dot((y * y).astype(BF16), same)
    return (y * lax.rsqrt(total * (1.0 / HEAD) + 1e-05)).astype(BF16)


def vmem_call(kernel, name, out_shape, operands, flops, scratch=(), spaces=None):
    spaces = spaces or {}
    specs = [
        pl.BlockSpec(memory_space=spaces.get(i, pltpu.VMEM)) for i in range(len(operands))
    ]
    count = sum(a.size * a.dtype.itemsize for a in operands)
    outs = jax.tree.map(lambda _: pl.BlockSpec(memory_space=pltpu.VMEM), out_shape)
    return pl.pallas_call(
        kernel,
        in_specs=specs,
        out_specs=outs,
        out_shape=out_shape,
        scratch_shapes=list(scratch),
        compiler_params=pltpu.CompilerParams(vmem_limit_bytes=16 << 20),
        cost_estimate=pl.CostEstimate(flops=flops, bytes_accessed=count, transcendentals=0),
        name=name,
    )(*operands)


def contract_last(a, b):
    return lax.dot_general(a, b, (((1,), (1,)), ((), ())), preferred_element_type=F32)


def split_kernel(tokens_ref, x_ref, low_ref, high_ref, *parts):
    x = tokens_ref[...]
    x_ref[...] = x
    for i, part in enumerate(parts):
        part[...] = x[i % 2 * WIN * WIN : (i % 2 + 1) * WIN * WIN]
    halves = x.astype(F32).reshape(-1, 2, WIN, D)
    low_ref[...] = halves[:, 0].reshape(-1, D).astype(BF16)
    high_ref[...] = halves[:, 1].reshape(-1, D).astype(BF16)


def plan_kernel(experts, shifts_ref, ids_ref, pack_ref, cells_ref, mask_ref, pick_ref):
    n = ids_ref.shape[1]
    shift_lat, shift_lon = shifts_ref[0], shifts_ref[1]
    cut_lat = WIN - shift_lat
    cut_lon = WIN - shift_lon
    expert = iota((experts, n), 0)
    hits = [ids_ref[k : k + 1, :] == expert for k in range(2)]
    both = jnp.where(hits[0] | hits[1], 1.0, 0.0)
    before = jnp.where(iota((n, n), 0) < iota((n, n), 1), 1.0, 0.0).astype(BF16)
    count = dot(both.astype(BF16), before)
    ranks = [jnp.sum(jnp.where(hit, count, 0.0), axis=0, keepdims=True) for hit in hits]
    ids = ids_ref[...].astype(F32)
    cell = iota((1, n), 1)
    flags = [
        jnp.where(flag, 1.0, 0.0)
        for flag in (cell >> 4 >= cut_lat, cell & 7 >= cut_lon, cell >> 3 >= cut_lat)
    ]
    lines = jnp.concatenate([ids, *ranks, *flags, jnp.zeros((1, n), F32)], axis=0)
    eye = jnp.where(iota((n, n), 0) == iota((n, n), 1), 1.0, 0.0).astype(BF16)
    cells = contract_last(eye, lines.astype(BF16))
    cells_ref[...] = cells
    slot = iota((MOST * experts, n), 0).astype(F32)
    codes = [ids[k : k + 1] * MOST + ranks[k] for k in range(2)]
    pack_ref[...] = jnp.where((slot == codes[0]) | (slot == codes[1]), 1.0, 0.0).astype(BF16)
    slot = iota((1, 2 * MOST * experts), 1)
    slot = (slot // (2 * MOST) * MOST + slot % MOST).astype(F32)
    for k in range(2):
        code = cells[:, k : k + 1] * MOST + cells[:, 2 + k : 3 + k]
        pick_ref[k * n : (k + 1) * n, :] = jnp.where(slot == code, 1.0, 0.0).astype(BF16)
    cell = iota((n, 1), 0)
    query = jnp.where(cell >> 4 >= cut_lat, 3, 0) + ((cell & 15) + shift_lon >> 3)
    key = iota((1, 3 * n), 1)
    narrow = key >= 2 * n
    halo_row = ((key >= n) & (key < 2 * n)) | (key >= 2 * n + WIN * WIN)
    past = jnp.where(narrow, key >> 3 & 7, key >> 4 & 7) >= cut_lat
    lat = lax.axis_index("lat")
    first, final = lat == 0, lat == lax.axis_size("lat") - 1
    beyond = halo_row & ((past & first) | (~past & final))
    window = jnp.where(past != halo_row, 3, 0) + jnp.where(
        narrow, jnp.where(key & 7 >= cut_lon, 0, 2), (key & 15) + shift_lon >> 3
    )
    valid = jnp.where(query == jnp.where(beyond, -1, window), 1.0, 0.0).astype(BF16)
    mask_ref[0:n, :] = valid
    mask_ref[n : 2 * n, :] = valid


def blocks(width):
    return [slice(i, i + width) for i in range(0, D, width)]


def keys_values(x, w_ref):
    keys = dot(x, w_ref[:, D : 2 * D]).astype(BF16).astype(F32)
    values = dot(x, w_ref[:, 2 * D :]).astype(BF16)
    return jnp.concatenate([head_norm(keys[:, lanes]) for lanes in blocks(BLK)], axis=1), values


def attend_keys(queries_ref, keys, values, mask, scale=None):
    n = queries_ref.shape[0] // 2
    low_half = iota((1, 128), 1) < HEAD
    pairs = blocks(128)
    ones = jnp.ones((keys.shape[0], 128), BF16)
    scores = [contract_last(queries_ref[:, lanes], keys[:, lanes]) for lanes in pairs]
    if scale is not None:
        scores = [
            jnp.concatenate(
                [score[0:n] * scale[2 * i : 2 * i + 1], score[n:] * scale[2 * i + 1 : 2 * i + 2]], axis=0
            )
            for i, score in enumerate(scores)
        ]
    weights = [jnp.exp(score).astype(BF16) * mask for score in scores]
    sums = [
        dot(weight, jnp.concatenate([values[:, lanes], ones], axis=1))
        for weight, lanes in zip(weights, pairs, strict=True)
    ]
    return [
        (
            jnp.where(low_half, both[0:n, 0:128], both[n:, 0:128]),
            jnp.where(low_half, both[0:n, 128:], both[n:, 128:]),
        )
        for both in sums
    ]


def own_kernel(x_ref, w_ref, qq_ref, k_ref, v_ref):
    n = x_ref.shape[0]
    x = rms(x_ref[...].astype(F32)).astype(BF16)
    queries = dot(x, w_ref[:, 0:D]).astype(BF16).astype(F32)
    k_ref[...], v_ref[...] = keys_values(x, w_ref)
    low_half = (iota((1, BLK), 1) & 127) < HEAD
    for lanes in blocks(BLK):
        q = head_norm(queries[:, lanes]).astype(F32) * 0.125
        qq_ref[0:n, lanes] = jnp.where(low_half, q, 0.0).astype(BF16)
        qq_ref[n:, lanes] = jnp.where(low_half, 0.0, q).astype(BF16)


def side_kernel(left_ref, right_ref, cells_ref, side_ref):
    n = side_ref.shape[0]
    side_ref[...] = jnp.where(
        cells_ref[0:n, 5:6] > 0.5, left_ref[...].astype(F32), right_ref[...].astype(F32)
    ).astype(BF16)


def near_kernel(
    up_ref, up_more_ref, down_ref, down_more_ref, side_ref, w_ref, mask_ref, cells_ref, qq_ref, k_ref,
    v_ref, num_ref, den_ref,
):
    up = jnp.concatenate([up_ref[...], up_more_ref[...]], axis=0).astype(F32)
    down = jnp.concatenate([down_ref[...], down_more_ref[...]], axis=0).astype(F32)
    band = jnp.where(cells_ref[:, 4:5] > 0.5, up, down)
    x = jnp.concatenate(
        [rms(band).astype(BF16), rms(side_ref[...].astype(F32)).astype(BF16)], axis=0
    )
    keys, values = keys_values(x, w_ref)
    keys = jnp.concatenate([k_ref[...], keys], axis=0)
    values = jnp.concatenate([v_ref[...], values], axis=0)
    sums = attend_keys(qq_ref, keys, values, mask_ref[:, 0 : keys.shape[0]])
    for lanes, (num, den) in zip(blocks(128), sums, strict=True):
        num_ref[:, lanes] = num
        den_ref[:, lanes] = den


def last_kernel(
    x_ref, up_ref, down_ref, w_ref, mask_ref, qq_ref, num_ref, den_ref,
    wo_ref, router_ref, cells_ref, pack_ref, mixed_ref, gates_ref, send_ref,
):
    n = x_ref.shape[0]
    m = up_ref.shape[0]
    past = cells_ref[0:m, 6:7] > 0.5
    corner = jnp.where(past, up_ref[...].astype(F32), down_ref[...].astype(F32))
    x = rms(corner).astype(BF16)
    keys = dot(x, w_ref[:, D : 2 * D]).astype(BF16)
    values = dot(x, w_ref[:, 2 * D :]).astype(BF16)
    heads = D // HEAD
    head = jnp.where(iota((heads, D), 0) == iota((heads, D), 1) // HEAD, 1.0, 0.0).astype(BF16)
    square = keys.astype(F32) * keys.astype(F32)
    scale = lax.rsqrt(contract_last(head, square.astype(BF16)) * (1.0 / HEAD) + 1e-05)
    sums = attend_keys(qq_ref, keys, values, mask_ref[:, 3 * n - m :], scale)
    attended = [
        ((num_ref[:, lanes] + num) / (den_ref[:, lanes] + den)).astype(BF16)
        for lanes, (num, den) in zip(blocks(128), sums, strict=True)
    ]
    total = dot(jnp.concatenate(attended, axis=1), wo_ref[...])
    mixed = (x_ref[...].astype(F32) + total).astype(BF16)
    mixed_ref[...] = mixed
    normed = rms(mixed.astype(F32)).astype(BF16)
    logits = contract_last(normed, router_ref[...])
    experts = logits.shape[1]
    expert = iota(logits.shape, 1).astype(F32)
    sig = [
        jax.nn.sigmoid(
            jnp.sum(jnp.where(cells_ref[:, k : k + 1] == expert, logits, 0.0), axis=1, keepdims=True)
        )
        for k in range(2)
    ]
    gates_ref[...] = jnp.where(iota((n, 128), 1) == 0, sig[0], sig[1]) / (sig[0] + sig[1])
    rows = dot(pack_ref[...], normed).astype(BF16).reshape(-1, 8, 128)
    rows = rows.reshape(experts, MOST, 8, 128)
    send_ref[:, 0] = rows
    send_ref[:, 1] = rows


def expert_kernel(rows_ref, wg_ref, wu_ref, wd_ref, out_ref):
    x = rows_ref[...].reshape(-1, D)
    gate = dot(x, wg_ref[...])
    upper = dot(x, wu_ref[...])
    hidden = (jax.nn.silu(gate) * upper).astype(BF16)
    out_ref[...] = dot(hidden, wd_ref[...]).astype(BF16).reshape(out_ref.shape)


def combine_kernel(back_ref, pick_ref, gates_ref, mixed_ref, out_ref):
    n = mixed_ref.shape[0]
    both = dot(pick_ref[...], back_ref[...].reshape(-1, D))
    moe = gates_ref[:, 0:1] * both[0:n] + gates_ref[:, 1:2] * both[n:]
    out_ref[...] = (mixed_ref[...].astype(F32) + moe).astype(BF16)


def moved(x, down, right):
    n_lat, n_lon = lax.axis_size("lat"), lax.axis_size("lon")
    pairs = [
        (i * n_lon + j, (i + down) % n_lat * n_lon + (j + right) % n_lon)
        for i in range(n_lat)
        for j in range(n_lon)
    ]
    return lax.ppermute(x, AXES, pairs)


def body(tokens, shifts, w_qkv, w_out, router, expert_ids, w_gate, w_up, w_down):
    rows, cols, width = tokens.shape
    n = rows * cols
    experts = router.shape[1]
    shape = jax.ShapeDtypeStruct
    half = shape((n // 2, width), BF16)
    x, low, high, *parts = vmem_call(
        split_kernel,
        "split",
        [shape((n, width), BF16), *[half] * 6],
        (tokens.reshape(n, width),),
        3 << 30,
    )
    rows_up, rows_down = parts[:2], parts[2:]
    left = moved(high, 0, 1)
    right = moved(low, 0, -1)
    above = [moved(part, 1, 0) for part in rows_up]
    below = [moved(part, -1, 0) for part in rows_down]
    whole = shape((n, width), BF16)
    qq, keys, values = vmem_call(
        own_kernel,
        "own",
        [shape((2 * n, width), BF16), whole, whole],
        (x, w_qkv),
        6 * n * width * width,
    )
    shifts, ids, keys = lax.optimization_barrier((shifts, expert_ids.reshape(n, 2).T, keys))
    pack, cells, mask, pick = vmem_call(
        functools.partial(plan_kernel, experts),
        "plan",
        [
            shape((MOST * experts, n), BF16),
            shape((n, 8), F32),
            shape((2 * n, 3 * n), BF16),
            shape((2 * n, 2 * MOST * experts), BF16),
        ],
        (shifts, ids),
        1 << 30,
        spaces={0: pltpu.SMEM},
    )
    side = vmem_call(side_kernel, "side", half, (left, right, cells), 1 << 10)
    up_side = moved(side, 1, 0)
    down_side = moved(side, -1, 0)
    num, den = vmem_call(
        near_kernel,
        "near",
        [shape((n, width), F32)] * 2,
        (*above, *below, side, w_qkv, mask, cells, qq, keys, values),
        8 * n * width * width,
    )
    mixed, gates, send = vmem_call(
        last_kernel,
        "last",
        [
            shape((n, width), BF16),
            shape((n, 128), F32),
            shape((experts, 2, MOST, 8, width // 8), BF16),
        ],
        (x, up_side, down_side, w_qkv, mask, qq, num, den, w_out, router.T, cells, pack),
        6 * n * width * width,
    )
    send = send.reshape(2 * experts * MOST, 8, width // 8)
    received = lax.all_to_all(send, AXES, split_axis=0, concat_axis=0, tiled=True)
    part = vmem_call(
        expert_kernel, "experts", shape(received.shape, BF16), (received, w_gate, w_up, w_down), 1 << 32
    )
    back = lax.all_to_all(part, AXES, split_axis=0, concat_axis=0, tiled=True)
    out = vmem_call(
        combine_kernel, "combine", shape((n, width), BF16), (back, pick, gates, mixed), 1 << 30
    )
    return out.reshape(rows, cols, width)


def solution(mesh):
    placed = (
        P("lat", "lon", None),
        P(),
        P(),
        P(),
        P(),
        P("lat", "lon", None, None),
        P(None, ("lat", "lon")),
        P(None, ("lat", "lon")),
        P(("lat", "lon"), None),
    )
    return jax.shard_map(
        body, mesh=mesh, in_specs=placed, out_specs=P("lat", "lon", None), check_vma=False
    )
```

```python
import functools

import jax
import jax.numpy as jnp
from jax import lax
from jax.experimental import pallas as pl
from jax.experimental.pallas import tpu as pltpu
from jax.sharding import PartitionSpec as P

HEAD = 64
WIN = 8
MOST = 6
D = 1024
BLK = 256
BF16 = jnp.bfloat16
F32 = jnp.float32
AXES = ("lat", "lon")


def iota(shape, dim):
    return lax.broadcasted_iota(jnp.int32, shape, dim)


def dot(a, b):
    return jnp.dot(a, b, preferred_element_type=F32)


def rms(x):
    return x * lax.rsqrt(jnp.mean(x * x, axis=-1, keepdims=True) + 1e-05)


def head_norm(y):
    n = y.shape[1]
    same = jnp.where(iota((n, n), 0) // HEAD == iota((n, n), 1) // HEAD, 1.0, 0.0).astype(BF16)
    total = dot((y * y).astype(BF16), same)
    return (y * lax.rsqrt(total * (1.0 / HEAD) + 1e-05)).astype(BF16)


def vmem_call(kernel, name, out_shape, operands, flops, scratch=(), spaces=None):
    spaces = spaces or {}
    specs = [
        pl.BlockSpec(memory_space=spaces.get(i, pltpu.VMEM)) for i in range(len(operands))
    ]
    count = sum(a.size * a.dtype.itemsize for a in operands)
    outs = jax.tree.map(lambda _: pl.BlockSpec(memory_space=pltpu.VMEM), out_shape)
    return pl.pallas_call(
        kernel,
        in_specs=specs,
        out_specs=outs,
        out_shape=out_shape,
        scratch_shapes=list(scratch),
        compiler_params=pltpu.CompilerParams(vmem_limit_bytes=16 << 20),
        cost_estimate=pl.CostEstimate(flops=flops, bytes_accessed=count, transcendentals=0),
        name=name,
    )(*operands)


def contract_last(a, b):
    return lax.dot_general(a, b, (((1,), (1,)), ((), ())), preferred_element_type=F32)


def split_kernel(tokens_ref, x_ref, low_ref, high_ref, *parts):
    x = tokens_ref[...]
    x_ref[...] = x
    for i, part in enumerate(parts):
        part[...] = x[i % 2 * WIN * WIN : (i % 2 + 1) * WIN * WIN]
    halves = x.astype(F32).reshape(-1, 2, WIN, D)
    low_ref[...] = halves[:, 0].reshape(-1, D).astype(BF16)
    high_ref[...] = halves[:, 1].reshape(-1, D).astype(BF16)


def plan_kernel(experts, shifts_ref, ids_ref, pack_ref, cells_ref, mask_ref, pick_ref):
    n = ids_ref.shape[1]
    shift_lat, shift_lon = shifts_ref[0], shifts_ref[1]
    cut_lat = WIN - shift_lat
    cut_lon = WIN - shift_lon
    expert = iota((experts, n), 0)
    hits = [ids_ref[k : k + 1, :] == expert for k in range(2)]
    both = jnp.where(hits[0] | hits[1], 1.0, 0.0)
    before = jnp.where(iota((n, n), 0) < iota((n, n), 1), 1.0, 0.0).astype(BF16)
    count = dot(both.astype(BF16), before)
    ranks = [jnp.sum(jnp.where(hit, count, 0.0), axis=0, keepdims=True) for hit in hits]
    ids = ids_ref[...].astype(F32)
    cell = iota((1, n), 1)
    flags = [
        jnp.where(flag, 1.0, 0.0)
        for flag in (cell >> 4 >= cut_lat, cell & 7 >= cut_lon, cell >> 3 >= cut_lat)
    ]
    lines = jnp.concatenate([ids, *ranks, *flags, jnp.zeros((1, n), F32)], axis=0)
    eye = jnp.where(iota((n, n), 0) == iota((n, n), 1), 1.0, 0.0).astype(BF16)
    cells = contract_last(eye, lines.astype(BF16))
    cells_ref[...] = cells
    slot = iota((MOST * experts, n), 0).astype(F32)
    codes = [ids[k : k + 1] * MOST + ranks[k] for k in range(2)]
    pack_ref[...] = jnp.where((slot == codes[0]) | (slot == codes[1]), 1.0, 0.0).astype(BF16)
    slot = iota((1, 2 * MOST * experts), 1)
    slot = (slot // (2 * MOST) * MOST + slot % MOST).astype(F32)
    for k in range(2):
        code = cells[:, k : k + 1] * MOST + cells[:, 2 + k : 3 + k]
        pick_ref[k * n : (k + 1) * n, :] = jnp.where(slot == code, 1.0, 0.0).astype(BF16)
    cell = iota((n, 1), 0)
    query = jnp.where(cell >> 4 >= cut_lat, 3, 0) + ((cell & 15) + shift_lon >> 3)
    key = iota((1, 3 * n), 1)
    narrow = key >= 2 * n
    halo_row = ((key >= n) & (key < 2 * n)) | (key >= 2 * n + WIN * WIN)
    past = jnp.where(narrow, key >> 3 & 7, key >> 4 & 7) >= cut_lat
    lat = lax.axis_index("lat")
    first, final = lat == 0, lat == lax.axis_size("lat") - 1
    beyond = halo_row & ((past & first) | (~past & final))
    window = jnp.where(past != halo_row, 3, 0) + jnp.where(
        narrow, jnp.where(key & 7 >= cut_lon, 0, 2), (key & 15) + shift_lon >> 3
    )
    valid = jnp.where(query == jnp.where(beyond, -1, window), 1.0, 0.0).astype(BF16)
    mask_ref[0:n, :] = valid
    mask_ref[n : 2 * n, :] = valid


def blocks(width):
    return [slice(i, i + width) for i in range(0, D, width)]


def keys_values(x, w_ref):
    keys = dot(x, w_ref[:, D : 2 * D]).astype(BF16).astype(F32)
    values = dot(x, w_ref[:, 2 * D :]).astype(BF16)
    return jnp.concatenate([head_norm(keys[:, lanes]) for lanes in blocks(BLK)], axis=1), values


def attend_keys(queries_ref, keys, values, mask, scale=None):
    n = queries_ref.shape[0] // 2
    low_half = iota((1, 128), 1) < HEAD
    pairs = blocks(128)
    ones = jnp.ones((keys.shape[0], 128), BF16)
    scores = [contract_last(queries_ref[:, lanes], keys[:, lanes]) for lanes in pairs]
    if scale is not None:
        scores = [
            jnp.concatenate(
                [score[0:n] * scale[2 * i : 2 * i + 1], score[n:] * scale[2 * i + 1 : 2 * i + 2]], axis=0
            )
            for i, score in enumerate(scores)
        ]
    weights = [jnp.exp(score).astype(BF16) * mask for score in scores]
    sums = [
        dot(weight, jnp.concatenate([values[:, lanes], ones], axis=1))
        for weight, lanes in zip(weights, pairs, strict=True)
    ]
    return [
        (
            jnp.where(low_half, both[0:n, 0:128], both[n:, 0:128]),
            jnp.where(low_half, both[0:n, 128:], both[n:, 128:]),
        )
        for both in sums
    ]


def own_kernel(x_ref, w_ref, qq_ref, k_ref, v_ref):
    n = x_ref.shape[0]
    x = rms(x_ref[...].astype(F32)).astype(BF16)
    queries = dot(x, w_ref[:, 0:D]).astype(BF16).astype(F32)
    k_ref[...], v_ref[...] = keys_values(x, w_ref)
    low_half = (iota((1, BLK), 1) & 127) < HEAD
    for lanes in blocks(BLK):
        q = head_norm(queries[:, lanes]).astype(F32) * 0.125
        qq_ref[0:n, lanes] = jnp.where(low_half, q, 0.0).astype(BF16)
        qq_ref[n:, lanes] = jnp.where(low_half, 0.0, q).astype(BF16)


def side_kernel(left_ref, right_ref, cells_ref, side_ref, lower_ref, upper_ref):
    n = side_ref.shape[0]
    side = jnp.where(
        cells_ref[0:n, 5:6] > 0.5, left_ref[...].astype(F32), right_ref[...].astype(F32)
    )
    side_ref[...] = side.astype(BF16)
    upper_ref[...] = side[0 : n - WIN].astype(BF16)
    lower_ref[...] = side[WIN:].astype(BF16)


def near_kernel(
    up_ref, up_more_ref, down_ref, down_more_ref, side_ref, w_ref, mask_ref, cells_ref, qq_ref, k_ref,
    v_ref, num_ref, den_ref,
):
    up = jnp.concatenate([up_ref[...], up_more_ref[...]], axis=0).astype(F32)
    down = jnp.concatenate([down_ref[...], down_more_ref[...]], axis=0).astype(F32)
    band = jnp.where(cells_ref[:, 4:5] > 0.5, up, down)
    x = jnp.concatenate(
        [rms(band).astype(BF16), rms(side_ref[...].astype(F32)).astype(BF16)], axis=0
    )
    keys, values = keys_values(x, w_ref)
    keys = jnp.concatenate([k_ref[...], keys], axis=0)
    values = jnp.concatenate([v_ref[...], values], axis=0)
    sums = attend_keys(qq_ref, keys, values, mask_ref[:, 0 : keys.shape[0]])
    for lanes, (num, den) in zip(blocks(128), sums, strict=True):
        num_ref[:, lanes] = num
        den_ref[:, lanes] = den


def last_kernel(
    x_ref, down_ref, up_ref, w_ref, mask_ref, qq_ref, num_ref, den_ref,
    wo_ref, router_ref, cells_ref, pack_ref, mixed_ref, gates_ref, send_ref,
):
    n = x_ref.shape[0]
    m = WIN * WIN
    past = cells_ref[0:m, 6:7] > 0.5
    row = jnp.zeros((WIN, D), F32)
    up = jnp.concatenate([row, up_ref[...].astype(F32)], axis=0)
    down = jnp.concatenate([down_ref[...].astype(F32), row], axis=0)
    corner = jnp.where(past, up, down)
    x = rms(corner).astype(BF16)
    keys = dot(x, w_ref[:, D : 2 * D]).astype(BF16)
    values = dot(x, w_ref[:, 2 * D :]).astype(BF16)
    heads = D // HEAD
    head = jnp.where(iota((heads, D), 0) == iota((heads, D), 1) // HEAD, 1.0, 0.0).astype(BF16)
    square = keys.astype(F32) * keys.astype(F32)
    scale = lax.rsqrt(contract_last(head, square.astype(BF16)) * (1.0 / HEAD) + 1e-05)
    sums = attend_keys(qq_ref, keys, values, mask_ref[:, 3 * n - m :], scale)
    attended = [
        ((num_ref[:, lanes] + num) / (den_ref[:, lanes] + den)).astype(BF16)
        for lanes, (num, den) in zip(blocks(128), sums, strict=True)
    ]
    total = dot(jnp.concatenate(attended, axis=1), wo_ref[...])
    mixed = (x_ref[...].astype(F32) + total).astype(BF16)
    mixed_ref[...] = mixed
    normed = rms(mixed.astype(F32)).astype(BF16)
    logits = contract_last(normed, router_ref[...])
    experts = logits.shape[1]
    expert = iota(logits.shape, 1).astype(F32)
    sig = [
        jax.nn.sigmoid(
            jnp.sum(jnp.where(cells_ref[:, k : k + 1] == expert, logits, 0.0), axis=1, keepdims=True)
        )
        for k in range(2)
    ]
    gates_ref[...] = jnp.where(iota((n, 128), 1) == 0, sig[0], sig[1]) / (sig[0] + sig[1])
    rows = dot(pack_ref[...], normed).astype(BF16).reshape(-1, 8, 128)
    rows = rows.reshape(experts, MOST, 8, 128)
    send_ref[:, 0] = rows
    send_ref[:, 1] = rows


def expert_kernel(rows_ref, wg_ref, wu_ref, wd_ref, out_ref):
    x = rows_ref[...].reshape(-1, D)
    gate = dot(x, wg_ref[...])
    upper = dot(x, wu_ref[...])
    hidden = (jax.nn.silu(gate) * upper).astype(BF16)
    out_ref[...] = dot(hidden, wd_ref[...]).astype(BF16).reshape(out_ref.shape)


def combine_kernel(back_ref, pick_ref, gates_ref, mixed_ref, out_ref):
    n = mixed_ref.shape[0]
    both = dot(pick_ref[...], back_ref[...].reshape(-1, D))
    moe = gates_ref[:, 0:1] * both[0:n] + gates_ref[:, 1:2] * both[n:]
    out_ref[...] = (mixed_ref[...].astype(F32) + moe).astype(BF16)


def moved(x, down, right):
    n_lat, n_lon = lax.axis_size("lat"), lax.axis_size("lon")
    pairs = [
        (i * n_lon + j, (i + down) % n_lat * n_lon + (j + right) % n_lon)
        for i in range(n_lat)
        for j in range(n_lon)
    ]
    return lax.ppermute(x, AXES, pairs)


def body(tokens, shifts, w_qkv, w_out, router, expert_ids, w_gate, w_up, w_down):
    rows, cols, width = tokens.shape
    n = rows * cols
    experts = router.shape[1]
    shape = jax.ShapeDtypeStruct
    half = shape((n // 2, width), BF16)
    x, low, high, *parts = vmem_call(
        split_kernel,
        "split",
        [shape((n, width), BF16), *[half] * 6],
        (tokens.reshape(n, width),),
        3 << 30,
    )
    rows_up, rows_down = parts[:2], parts[2:]
    left = moved(high, 0, 1)
    right = moved(low, 0, -1)
    above = [moved(part, 1, 0) for part in rows_up]
    below = [moved(part, -1, 0) for part in rows_down]
    whole = shape((n, width), BF16)
    qq, keys, values = vmem_call(
        own_kernel,
        "own",
        [shape((2 * n, width), BF16), whole, whole],
        (x, w_qkv),
        6 * n * width * width,
    )
    shifts, ids, keys = lax.optimization_barrier((shifts, expert_ids.reshape(n, 2).T, keys))
    pack, cells, mask, pick = vmem_call(
        functools.partial(plan_kernel, experts),
        "plan",
        [
            shape((MOST * experts, n), BF16),
            shape((n, 8), F32),
            shape((2 * n, 3 * n), BF16),
            shape((2 * n, 2 * MOST * experts), BF16),
        ],
        (shifts, ids),
        1 << 30,
        spaces={0: pltpu.SMEM},
    )
    most = shape((WIN * WIN - WIN, width), BF16)
    side, lower, upper = vmem_call(
        side_kernel, "side", [half, most, most], (left, right, cells), 1 << 10
    )
    up_side = moved(lower, 1, 0)
    down_side = moved(upper, -1, 0)
    num, den = vmem_call(
        near_kernel,
        "near",
        [shape((n, width), F32)] * 2,
        (*above, *below, side, w_qkv, mask, cells, qq, keys, values),
        8 * n * width * width,
    )
    mixed, gates, send = vmem_call(
        last_kernel,
        "last",
        [
            shape((n, width), BF16),
            shape((n, 128), F32),
            shape((experts, 2, MOST, 8, width // 8), BF16),
        ],
        (x, down_side, up_side, w_qkv, mask, qq, num, den, w_out, router.T, cells, pack),
        6 * n * width * width,
    )
    send = send.reshape(2 * experts * MOST, 8, width // 8)
    received = lax.all_to_all(send, AXES, split_axis=0, concat_axis=0, tiled=True)
    part = vmem_call(
        expert_kernel, "experts", shape(received.shape, BF16), (received, w_gate, w_up, w_down), 1 << 32
    )
    back = lax.all_to_all(part, AXES, split_axis=0, concat_axis=0, tiled=True)
    out = vmem_call(
        combine_kernel, "combine", shape((n, width), BF16), (back, pick, gates, mixed), 1 << 30
    )
    return out.reshape(rows, cols, width)


def solution(mesh):
    placed = (
        P("lat", "lon", None),
        P(),
        P(),
        P(),
        P(),
        P("lat", "lon", None, None),
        P(None, ("lat", "lon")),
        P(None, ("lat", "lon")),
        P(("lat", "lon"), None),
    )
    return jax.shard_map(
        body, mesh=mesh, in_specs=placed, out_specs=P("lat", "lon", None), check_vma=False
    )
```
